256 devices in a mesh: ctx: 64 (over z, x_hi, y), head: 4 (over x_lo, core).
Axes of the slice: x: 4 (x_hi: 2, x_lo: 2; x = x_hi * 2 + x_lo), y: 4, z: 8, core: 2. Of those that a mesh axis runs over, the one named last changes fastest.
Arguments:
- queries: bfloat16 [16384, 4096], P(('ctx', 'head')), may hold values from -6 to 6
- keys: bfloat16 [16384, 512], P(('ctx', 'head')), may hold values from -6 to 6
- values: bfloat16 [16384, 512], P(('ctx', 'head')), may hold values from -6 to 6
- out_grad: bfloat16 [16384, 4096], P(('ctx', 'head')), may hold values from -6 to 6
- lse: float32 [16384, 32], P('ctx', 'head'), may hold values from 4.5 to 5.5
- delta: float32 [16384, 32], P('ctx', 'head'), may hold values from -15 to 15
- gate_block: int32 [32, 32], replicated, may hold values from 0 to 30, as said below
Outputs:
- grad_queries: bfloat16 [16384, 4096], P(('ctx', 'head'))
- key_gradient: bfloat16 [16384, 512], P(('ctx', 'head'))
- value_gradient: bfloat16 [16384, 512], P(('ctx', 'head'))
The draws below stay inside these ranges and needn't reach their ends.
Inputs may be any that keep to these rules, and one draw needn't show every extreme that they name: gate_block[b, h] is 0 for b = 0 and lies below b for every later block b.
All inputs are finite; a program needn't handle non-finite values.
Results may differ from the reference program's by a relative error of at most 0.0049.
Values may be sent and summed in bfloat16 or wider, within the bound.
A program may use at most 64 MiB of HBM per device.

```python
import math
import jax
import jax.numpy as jnp
from jax import lax

QUERY_HEADS = 32
KEY_VALUE_HEADS = 4
HEAD_SIZE = 128
KEY_BLOCK_TOKENS = 512
SEQUENCE_TOKENS = 16384


def draw_gate_block(key, part):
    key = jax.random.fold_in(key, 7)
    key_block_count = SEQUENCE_TOKENS // KEY_BLOCK_TOKENS
    key_one, key_two, key_three = jax.random.split(key, 3)
    draw_one = jax.random.randint(key_one, (key_block_count, QUERY_HEADS), 0, key_block_count)
    draw_two = jax.random.randint(key_two, (key_block_count, QUERY_HEADS), 0, key_block_count)
    block_index = jnp.arange(key_block_count, dtype=jnp.int32)[:, None]
    window = jnp.maximum(block_index, 1)
    distance = jnp.minimum(draw_one % window, draw_two % window)
    selected = jnp.where(block_index > 0, block_index - 1 - distance, 0)
    marked_head = jax.random.randint(key_three, (), 0, QUERY_HEADS)
    forced = (block_index == key_block_count - 1) & (jnp.arange(QUERY_HEADS, dtype=jnp.int32)[None, :] == marked_head)
    return jnp.where(forced, key_block_count - 2, selected).astype(jnp.int32)


def steps_of(own_key, extent, pieces, smallest, high):
    def one(dim, blocks):
        heights = jax.random.uniform(jax.random.fold_in(jax.random.fold_in(own_key, 6), dim), (blocks,), jnp.float32, smallest / len(pieces), high / len(pieces))
        return jnp.repeat(jnp.exp(heights), extent[dim] // blocks).reshape((-1,) + (1,) * (len(extent) - dim - 1))

    level = one(*pieces[0])
    for cut in pieces[1:]:
        level = level * one(*cut)
    return level


def centred(own_key, shape, width, most, shards=(), held_as=jnp.bfloat16):
    drawn = width * jax.random.normal(own_key, shape, jnp.float32)
    if shards:
        drawn = drawn * steps_of(own_key, shape, shards, -0.22, 0.18)
    return jnp.clip(drawn, -most, most).astype(held_as)


def setup_inputs(seed: int = 0) -> dict:
    key_of = jax.random.split(jax.random.key(seed), 8)
    return {
        "queries": centred(key_of[0], (SEQUENCE_TOKENS, QUERY_HEADS * HEAD_SIZE), 1.0, 6.0, ((0, 256),)),
        "keys": centred(key_of[1], (SEQUENCE_TOKENS, KEY_VALUE_HEADS * HEAD_SIZE), 1.0, 6.0, ((0, 256),)),
        "values": centred(key_of[2], (SEQUENCE_TOKENS, KEY_VALUE_HEADS * HEAD_SIZE), 1.0, 6.0, ((0, 256),)),
        "out_grad": centred(key_of[3], (SEQUENCE_TOKENS, QUERY_HEADS * HEAD_SIZE), 1.0, 6.0, ((0, 256),)),
        "lse": jnp.clip(4.5 + 1.0 * jax.random.uniform(key_of[4], (SEQUENCE_TOKENS, QUERY_HEADS), jnp.float32) ** steps_of(key_of[4], (SEQUENCE_TOKENS, QUERY_HEADS), ((0, 64), (1, 4)), -0.2, 0.2), 4.5, 5.5),
        "delta": centred(key_of[5], (SEQUENCE_TOKENS, QUERY_HEADS), 3.0, 15.0, ((0, 64), (1, 4)), jnp.float32),
        "gate_block": draw_gate_block(jax.random.fold_in(key_of[7], 71), 0),
    }


def block_terms(q_rows, o_rows, l_rows, d_rows, k_heads, v_heads, visible, score_scale):
    scores = jnp.einsum('rhd,htd->hrt', q_rows.astype(jnp.float32), k_heads.astype(jnp.float32)) * score_scale
    weights = jnp.where(visible, jnp.exp(scores - l_rows.T[:, :, None]), 0.0)
    grad_weights = jnp.einsum('rhd,htd->hrt', o_rows.astype(jnp.float32), v_heads.astype(jnp.float32))
    grad_scores = weights * (grad_weights - d_rows.T[:, :, None])
    weights_low = lax.optimization_barrier(weights.astype(jnp.bfloat16)).astype(jnp.float32)
    slopes_low = lax.optimization_barrier(grad_scores.astype(jnp.bfloat16)).astype(jnp.float32)
    grad_q = jnp.einsum('hrt,htd->rhd', slopes_low, k_heads.astype(jnp.float32)) * score_scale
    grad_k = jnp.einsum('hrt,rhd->htd', slopes_low, q_rows.astype(jnp.float32)) * score_scale
    grad_v = jnp.einsum('hrt,rhd->htd', weights_low, o_rows.astype(jnp.float32))
    return (grad_q, grad_k, grad_v)

def reference(queries, keys, values, out_grad, lse, delta, gate_block):
    key_block_count = SEQUENCE_TOKENS // KEY_BLOCK_TOKENS
    heads_per_group = QUERY_HEADS // KEY_VALUE_HEADS
    score_scale = 1.0 / math.sqrt(HEAD_SIZE)
    q_blocks = queries.reshape(key_block_count, KEY_BLOCK_TOKENS, QUERY_HEADS, HEAD_SIZE)
    o_blocks = out_grad.reshape(key_block_count, KEY_BLOCK_TOKENS, QUERY_HEADS, HEAD_SIZE)
    blocked_keys = keys.reshape(key_block_count, KEY_BLOCK_TOKENS, KEY_VALUE_HEADS, HEAD_SIZE)
    blocked_values = values.reshape(key_block_count, KEY_BLOCK_TOKENS, KEY_VALUE_HEADS, HEAD_SIZE)
    l_blocks = lse.reshape(key_block_count, KEY_BLOCK_TOKENS, QUERY_HEADS)
    d_blocks = delta.reshape(key_block_count, KEY_BLOCK_TOKENS, QUERY_HEADS)
    kv_head = jnp.arange(QUERY_HEADS, dtype=jnp.int32) // heads_per_group
    positions = jnp.arange(KEY_BLOCK_TOKENS, dtype=jnp.int32)
    causal = (positions[:, None] >= positions[None, :])[None]

    def one_block(totals, index):
        key_gradient_sum, value_gradient_sum = totals
        q_rows = q_blocks[index]
        o_rows = o_blocks[index]
        l_rows = l_blocks[index]
        d_rows = d_blocks[index]
        own_k = jnp.transpose(blocked_keys[index][:, kv_head, :], (1, 0, 2))
        own_v = jnp.transpose(blocked_values[index][:, kv_head, :], (1, 0, 2))
        own_q, local_key_gradient, local_value_gradient = block_terms(q_rows, o_rows, l_rows, d_rows, own_k, own_v, causal, score_scale)
        gates = gate_block[index]
        gate_k = blocked_keys[gates, :, kv_head]
        gate_v = blocked_values[gates, :, kv_head]
        other = (gates != index)[:, None, None]
        gate_q, gate_kg, gate_vg = block_terms(q_rows, o_rows, l_rows, d_rows, gate_k, gate_v, other, score_scale)
        local_key_gradient = jnp.transpose(local_key_gradient.reshape(KEY_VALUE_HEADS, heads_per_group, KEY_BLOCK_TOKENS, HEAD_SIZE).sum(axis=1), (1, 0, 2))
        local_value_gradient = jnp.transpose(local_value_gradient.reshape(KEY_VALUE_HEADS, heads_per_group, KEY_BLOCK_TOKENS, HEAD_SIZE).sum(axis=1), (1, 0, 2))
        key_gradient_sum = key_gradient_sum.at[index].add(local_key_gradient)
        value_gradient_sum = value_gradient_sum.at[index].add(local_value_gradient)
        key_gradient_sum = key_gradient_sum.at[gates, :, kv_head].add(gate_kg)
        value_gradient_sum = value_gradient_sum.at[gates, :, kv_head].add(gate_vg)
        return ((key_gradient_sum, value_gradient_sum), own_q + gate_q)
    zero_filled = jnp.zeros((key_block_count, KEY_BLOCK_TOKENS, KEY_VALUE_HEADS, HEAD_SIZE), jnp.float32)
    (key_gradient_sum, value_gradient_sum), query_total = lax.scan(one_block, (zero_filled, zero_filled), jnp.arange(key_block_count, dtype=jnp.int32))
    grad_queries = query_total.reshape(SEQUENCE_TOKENS, QUERY_HEADS * HEAD_SIZE).astype(jnp.bfloat16)
    key_gradient = key_gradient_sum.reshape(SEQUENCE_TOKENS, KEY_VALUE_HEADS * HEAD_SIZE).astype(jnp.bfloat16)
    value_gradient = value_gradient_sum.reshape(SEQUENCE_TOKENS, KEY_VALUE_HEADS * HEAD_SIZE).astype(jnp.bfloat16)
    return (grad_queries, key_gradient, value_gradient)
```

```python
import math

import jax
import jax.numpy as jnp
from jax import lax
from jax.experimental import pallas as pl
from jax.experimental.pallas import tpu as pltpu
from jax.sharding import PartitionSpec as P

MESH = pl.DeviceIdType.MESH
LOG2E = math.log2(math.e)
SCALE = 1.0 / math.sqrt(128.0)
F32 = jnp.float32
BF16 = jnp.bfloat16


def flip(bit, by):
    return bit if by == 0 else 1 - bit


def xor(a, b):
    return lax.rem(a + b, 2)


class Place:
    def __init__(self):
        ctx, head = lax.axis_index("ctx"), lax.axis_index("head")
        self.z = ctx // 8
        self.X = lax.rem(ctx // 4, 2)
        self.Y = lax.rem(ctx // 2, 2)
        self.yl = lax.rem(ctx, 2)
        self.xl = head // 2
        self.c = lax.rem(head, 2)
        self.gx, self.gy = xor(self.xl, self.X), xor(self.yl, self.Y)
        self.g = self.gx * 2 + self.gy
        self.e = self.g * 2 + self.c
        self.s = self.yl * 4 + self.xl * 2 + self.c
        self.m = self.X * 4 + self.Y * 2 + self.c
        self.b = self.z * 4 + self.X * 2 + self.Y

    def inner(self, k):
        yl, xl, c = flip(self.yl, k // 4), flip(self.xl, k // 2 % 2), flip(self.c, k % 2)
        e = (xor(xl, self.X) * 2 + xor(yl, self.Y)) * 2 + c
        return device(self.z, self.X, xl, self.Y, yl, c), yl * 4 + xl * 2 + c, e

    def row(self, k):
        X, Y, c = flip(self.X, k // 4), flip(self.Y, k // 2 % 2), flip(self.c, k % 2)
        return device(self.z, X, xor(self.gx, X), Y, xor(self.gy, Y), c), X * 4 + Y * 2 + c

    def above(self):
        return {"ctx": lax.rem(self.z + 1, 8) * 8 + self.X * 4 + self.Y * 2 + self.yl}

    def below(self):
        return {"ctx": lax.rem(self.z + 7, 8) * 8 + self.X * 4 + self.Y * 2 + self.yl}

    def barrier_signal(self, sem):
        for k in range(1, 32):
            to = device(
                self.z,
                flip(self.X, k // 16),
                flip(self.xl, k // 8 % 2),
                flip(self.Y, k // 4 % 2),
                flip(self.yl, k // 2 % 2),
                flip(self.c, k % 2),
            )
            pl.semaphore_signal(sem, inc=1, device_id=to, device_id_type=MESH)
        for to in (self.above(), self.below()):
            pl.semaphore_signal(sem, inc=1, device_id=to, device_id_type=MESH)


BARRIER_COUNT = 33


def device(z, X, xl, Y, yl, c):
    return {"ctx": z * 8 + X * 4 + Y * 2 + yl, "head": xl * 2 + c}


def remote(src, dst, send, recv, to):
    return pltpu.make_async_remote_copy(
        src_ref=src, dst_ref=dst, send_sem=send, recv_sem=recv, device_id=to, device_id_type=MESH
    )


def ring_steps():
    return [(t, h) for t in range(3) for h in range(2)]


def gather_kernel(
    tab,
    q_ref,
    o_ref,
    k_ref,
    v_ref,
    ld_ref,
    q_in,
    o_in,
    own_kv,
    gkv,
    ld_in,
    kvl,
    kvz,
    picked,
    q_send,
    q_recv,
    ld_send,
    ld_recv,
    p_send,
    p_recv,
    z_send,
    z_recv,
    r_send,
    r_recv,
    l_sem,
):
    me = Place()
    barrier = pltpu.get_barrier_semaphore()
    me.barrier_signal(barrier)
    for g in range(4):
        kvl[g, :, :128] = k_ref[:, g * 128 : (g + 1) * 128]
        kvl[g, :, 128:] = v_ref[:, g * 128 : (g + 1) * 128]
    pl.semaphore_wait(barrier, BARRIER_COUNT)

    staying = (me.xl == me.X) & (me.yl == me.Y)
    sends = []
    for g in range(4):
        X, Y = me.xl, me.yl
        to = device(me.z, X, xor(X, g // 2), Y, xor(Y, g % 2), me.c)
        copy = remote(kvl.at[g], kvz.at[me.b], p_send.at[g], p_recv.at[me.X * 2 + me.Y], to)
        if g == 0:

            @pl.when(staying)
            def _():
                kvz[me.b] = kvl[0]

            @pl.when(jnp.logical_not(staying))
            def _():
                copy.start()
        else:
            copy.start()
        sends.append(copy)

    mine = []
    for k in range(1, 8):
        to, _, e = me.inner(k)
        mine.append(remote(kvl.at[e // 2], own_kv.at[me.s], q_send.at[2, k], q_recv.at[2, k], to))
        mine[-1].start()
    for k in range(1, 8):
        to, _, e = me.inner(k)
        cols = pl.ds(pl.multiple_of(e * 512, 512), 512)
        for i, (src, dst) in enumerate(((q_ref, q_in), (o_ref, o_in))):
            mine.append(
                remote(src.at[:, cols], dst.at[me.s], q_send.at[i, k], q_recv.at[i, k], to)
            )
            mine[-1].start()
    cols = pl.ds(pl.multiple_of(me.e * 512, 512), 512)
    local = [
        pltpu.make_async_copy(src.at[:, cols], dst.at[me.s], l_sem.at[i])
        for i, (src, dst) in enumerate(((q_ref, q_in), (o_ref, o_in)))
    ]
    for copy in local:
        copy.start()
    own_kv[me.s] = kvl[me.g]

    ld_yl = xor(me.c, me.Y)
    ld_xl = xor(me.xl, me.X)
    ld_copies = []
    for core in range(2):
        to = device(me.z, me.X, ld_xl, me.Y, ld_yl, core)
        here = (ld_xl == me.xl) & (ld_yl == me.yl) & (me.c == core)
        copy = remote(ld_ref, ld_in.at[me.yl], ld_send.at[core], ld_recv.at[me.yl], to)

        @pl.when(here)
        def _():
            ld_in[me.yl] = ld_ref[...]

        @pl.when(jnp.logical_not(here))
        def _():
            copy.start()

        ld_copies.append((here, copy))

    def chunk(d, half):
        return kvz.at[pl.ds(lax.rem(d + 8, 8) * 4 + half * 2, 2)]

    ring = []

    def pass_on(way, t, half):
        d = me.z - t if way == 0 else me.z + t
        part = chunk(d, half)
        copy = remote(
            part,
            part,
            z_send.at[way, t, half],
            z_recv.at[way, t, half],
            me.above() if way == 0 else me.below(),
        )
        copy.start()
        ring.append(copy)

    def arrived(way, t, half):
        d = me.z - t - 1 if way == 0 else me.z + t + 1
        part = chunk(d, half)
        remote(
            part, part, z_send.at[way, t, half], z_recv.at[way, t, half], me.above()
        ).wait_recv()

    for half in range(2):
        for Y in range(2):
            w = half * 2 + Y
            here = staying & (me.X * 2 + me.Y == w)
            block = kvz.at[me.z * 4 + w]

            @pl.when(jnp.logical_not(here))
            def _():
                remote(block, block, p_send.at[0], p_recv.at[w], me.above()).wait_recv()

        for way in range(2):
            pass_on(way, 0, half)
    for t in range(1, 4):
        for half in range(2):
            for way in range(2):
                arrived(way, t - 1, half)
                if t < 3 or half == way:
                    pass_on(way, t, half)
    for way in range(2):
        arrived(way, 3, way)

    rows = []
    for k in (7, 6, 5, 4, 3, 2, 1, 0):
        to, p = me.row(k)
        for h in range(4):
            got = kvz[tab[0, p * 4 + h]]
            if k == 0:
                gkv[me.m, h] = got
            else:
                picked[k, h] = got
        if k:
            copy = remote(picked.at[k], gkv.at[me.m], r_send.at[k], r_recv.at[k], to)
            copy.start()
            rows.append(copy)

    for copy in local:
        copy.wait()
    for copy in mine:
        copy.wait_send()
    for k in range(1, 8):
        _, s, _ = me.inner(k)
        for i, dst in enumerate((q_in, o_in, own_kv)):
            part = dst.at[s]
            remote(part, part, q_send.at[i, k], q_recv.at[i, k], me.above()).wait_recv()
    for here, copy in ld_copies:

        @pl.when(jnp.logical_not(here))
        def _():
            copy.wait_send()

    for yl in range(2):
        here = (me.gx == me.xl) & (me.gy == me.c) & (me.yl == yl)
        part = ld_in.at[yl]

        @pl.when(jnp.logical_not(here))
        def _():
            remote(part, part, ld_send.at[0], ld_recv.at[yl], me.above()).wait_recv()

    @pl.when(jnp.logical_not(staying))
    def _():
        sends[0].wait_send()

    for copy in sends[1:] + ring + rows:
        copy.wait_send()
    for k in range(1, 8):
        _, p = me.row(k)
        part = gkv.at[p]
        remote(part, part, r_send.at[k], r_recv.at[k], me.above()).wait_recv()


def dot(a, b, contract):
    return lax.dot_general(a, b, ((contract[:1], contract[1:]), ((), ())), preferred_element_type=F32)


def terms(q, o, lse, delta, k, v, mask):
    scores = dot(k, q, (1, 1)) * (SCALE * LOG2E)
    weights = jnp.exp2(scores - lse)
    if mask is not None:
        weights = jnp.where(mask, weights, 0.0)
    slopes = weights * (dot(v, o, (1, 1)) - delta)
    return weights.astype(BF16), slopes.astype(BF16)


def attend_kernel(tab, q_in, o_in, own_kv, gkv, ld_in, dq_out, own_out, gate_out):
    me = Place()
    tile = 256
    key_pos = lax.broadcasted_iota(jnp.int32, (tile, tile), 0)
    query_pos = lax.broadcasted_iota(jnp.int32, (tile, tile), 1)
    causal = key_pos <= query_pos
    own = own_kv[...].reshape(512, 256)
    own_k, own_v = own[:, :128], own[:, 128:]
    own_dk = [jnp.zeros((tile, 128), F32) for _ in range(2)]
    own_dv = [jnp.zeros((tile, 128), F32) for _ in range(2)]
    for h in range(4):
        lanes = slice(h * 128, (h + 1) * 128)
        q = q_in[:, :, lanes].reshape(512, 128)
        o = o_in[:, :, lanes].reshape(512, 128)
        row = 4 * me.c + h
        lse = jnp.concatenate([ld_in[i, pl.ds(row, 1), :] for i in range(2)], axis=1) * LOG2E
        delta = jnp.concatenate([ld_in[i, pl.ds(row + 8, 1), :] for i in range(2)], axis=1)
        gate_on = tab[0, me.m * 4 + h] != me.b
        gate_lse = jnp.where(gate_on, lse, 1e30)
        gk = gkv[:, h, :, :128].reshape(512, 128)
        gv = gkv[:, h, :, 128:].reshape(512, 128)
        gdk = [jnp.zeros((tile, 128), F32) for _ in range(2)]
        gdv = [jnp.zeros((tile, 128), F32) for _ in range(2)]
        for i in range(2):
            cols = slice(i * tile, (i + 1) * tile)
            qi, oi, di = q[cols], o[cols], delta[:, cols]
            dq = jnp.zeros((tile, 128), F32)
            for j in range(2):
                keys = slice(j * tile, (j + 1) * tile)
                w, s = terms(qi, oi, gate_lse[:, cols], di, gk[keys], gv[keys], None)
                gdv[j] += dot(w, oi, (1, 0))
                gdk[j] += dot(s, qi, (1, 0))
                dq += dot(s, gk[keys], (0, 0))
            for j in range(i + 1):
                keys = slice(j * tile, (j + 1) * tile)
                mask = causal if i == j else None
                w, s = terms(qi, oi, lse[:, cols], di, own_k[keys], own_v[keys], mask)
                own_dv[j] += dot(w, oi, (1, 0))
                own_dk[j] += dot(s, qi, (1, 0))
                dq += dot(s, own_k[keys], (0, 0))
            dq_out[i * 4 : (i + 1) * 4, :, lanes] = (dq * SCALE).astype(BF16).reshape(4, 64, 128)
        for j in range(2):
            part = jnp.concatenate([gdk[j] * SCALE, gdv[j]], axis=1).astype(BF16)
            gate_out[j * 4 : (j + 1) * 4, h] = part.reshape(4, 64, 256)
    for j in range(2):
        part = jnp.concatenate([own_dk[j] * SCALE, own_dv[j]], axis=1).astype(BF16)
        own_out[j * 4 : (j + 1) * 4] = part.reshape(4, 64, 256)


def scatter_kernel(
    tab,
    dq_ref,
    own_ref,
    gate_ref,
    out_q,
    out_k,
    out_v,
    own_in,
    gate_in,
    run,
    z_out,
    z_in,
    sum_out,
    sum_in,
    q_send,
    q_recv,
    r_send,
    r_recv,
    z_send,
    z_recv,
    p_send,
    p_recv,
    l_sem,
):
    me = Place()
    barrier = pltpu.get_barrier_semaphore()
    me.barrier_signal(barrier)
    gate_in[me.m] = gate_ref[me.m]
    own_in[me.e] = own_ref[me.s]
    run[32] = jnp.zeros((64, 256), F32)
    pl.semaphore_wait(barrier, BARRIER_COUNT)

    copies = []
    for k in (7, 6, 5, 4, 3, 2, 1):
        to, p = me.row(k)
        copies.append(remote(gate_ref.at[p], gate_in.at[me.m], r_send.at[k], r_recv.at[k], to))
        copies[-1].start()
    cols = pl.ds(pl.multiple_of(me.e * 512, 512), 512)
    for k in range(1, 8):
        to, s, _ = me.inner(k)
        copies.append(remote(dq_ref.at[s], out_q.at[:, cols], q_send.at[0, k], q_recv.at[0, k], to))
        copies[-1].start()
        copies.append(remote(own_ref.at[s], own_in.at[me.e], q_send.at[1, k], q_recv.at[1, k], to))
        copies[-1].start()
    local = pltpu.make_async_copy(dq_ref.at[me.s], out_q.at[:, cols], l_sem)
    local.start()

    for k in range(1, 8):
        _, p = me.row(k)
        part = gate_in.at[p]
        remote(part, part, r_send.at[k], r_recv.at[k], me.above()).wait_recv()

    def add(i, carry):
        run[i] = gate_in[i // 4, lax.rem(i, 4)].astype(F32) + run[tab[1, i]]
        return carry

    lax.fori_loop(0, 32, add, 0)

    def total(d, w):
        return run[tab[2, lax.rem(d + 8, 8) * 4 + w]]

    for t in range(4):
        for half in range(2):
            for way in range(2):
                if t == 0 and half != way:
                    continue
                d = me.z + 4 - t if way == 0 else me.z - 4 + t
                to = me.above() if way == 0 else me.below()
                if t >= 2 or (t == 1 and half == way):
                    part = z_in.at[way, t - 1, half]
                    remote(
                        part, part, z_send.at[way, t - 1, half], z_recv.at[way, t - 1, half], to
                    ).wait_recv()
                for i in range(2):
                    value = total(d, half * 2 + i)
                    if t >= 2 or (t == 1 and half == way):
                        value += z_in[way, t - 1, half, i].astype(F32)
                    z_out[way, t, half, i] = value.astype(BF16)
                copy = remote(
                    z_out.at[way, t, half],
                    z_in.at[way, t, half],
                    z_send.at[way, t, half],
                    z_recv.at[way, t, half],
                    to,
                )
                copy.start()
                copies.append(copy)
    staying = (me.xl == me.X) & (me.yl == me.Y)
    ends = []
    for half in range(2):
        for way in range(2):
            part = z_in.at[way, 3, half]
            remote(
                part, part, z_send.at[way, 3, half], z_recv.at[way, 3, half], me.above()
            ).wait_recv()
        for i in range(2):
            w = half * 2 + i
            value = total(me.z, w)
            for way in range(2):
                value += z_in[way, 3, half, i].astype(F32)
            sum_out[w] = value.astype(BF16)
            here = staying & (me.X * 2 + me.Y == w)
            to = device(me.z, w // 2, me.X, w % 2, me.Y, me.c)
            copy = remote(sum_out.at[w], sum_in.at[me.g], p_send.at[w], p_recv.at[me.g], to)

            @pl.when(here)
            def _():
                sum_in[0] = sum_out[w]

            @pl.when(jnp.logical_not(here))
            def _():
                copy.start()

            ends.append((here, copy))

    for k in range(1, 8):
        _, s, e = me.inner(k)
        part = own_in.at[e]
        remote(part, part, q_send.at[1, k], q_recv.at[1, k], me.above()).wait_recv()
    for g in range(4):
        part = sum_in.at[g]
        copy = remote(part, part, p_send.at[g], p_recv.at[g], me.above())
        if g == 0:

            @pl.when(jnp.logical_not(staying))
            def _():
                copy.wait_recv()
        else:
            copy.wait_recv()
        value = sum_in[g].astype(F32) + own_in[2 * g].astype(F32) + own_in[2 * g + 1].astype(F32)
        out_k[:, g * 128 : (g + 1) * 128] = value[:, :128].astype(BF16)
        out_v[:, g * 128 : (g + 1) * 128] = value[:, 128:].astype(BF16)

    local.wait()
    for k in range(1, 8):
        _, s, e = me.inner(k)
        part = out_q.at[:, pl.ds(pl.multiple_of(e * 512, 512), 512)]
        remote(part, part, q_send.at[0, k], q_recv.at[0, k], me.above()).wait_recv()
    for here, copy in ends:

        @pl.when(jnp.logical_not(here))
        def _():
            copy.wait_send()

    for copy in copies:
        copy.wait_send()


def vmem(count):
    return [pl.BlockSpec(memory_space=pltpu.VMEM)] * count


SMEM_SPEC = pl.BlockSpec(memory_space=pltpu.SMEM)
ANY_SPEC = pl.BlockSpec(memory_space=pl.ANY)
DMA = pltpu.SemaphoreType.DMA
VMEM_LIMIT = 48 * 1024 * 1024


def shape(*dims, dtype=BF16):
    return jax.ShapeDtypeStruct(dims, dtype)


def shards(queries, keys, values, out_grad, lse, delta, gate_block):
    ctx, head = lax.axis_index("ctx"), lax.axis_index("head")
    z, X, Y, yl, xl = ctx // 8, ctx // 4 % 2, ctx // 2 % 2, ctx % 2, head // 2
    g = (xl + X) % 2 * 2 + (yl + Y) % 2
    gates = lax.dynamic_slice(gate_block, (z * 4, g * 8), (4, 8)).reshape(32)
    slots = jnp.arange(32, dtype=jnp.int32)
    same = (gates[:, None] == gates[None, :]) & (slots[None, :] < slots[:, None])
    previous = jnp.max(jnp.where(same, slots[None, :], -1), axis=1)
    member = gates[None, :] == slots[:, None]
    last = jnp.max(jnp.where(member, slots[None, :], -1), axis=1)
    tab = jnp.stack([gates, jnp.where(previous < 0, 32, previous), jnp.where(last < 0, 32, last)])
    ld = jnp.concatenate([lse.T, delta.T], axis=0)

    q_in, o_in, own_kv, gkv, ld_in = pl.pallas_call(
        gather_kernel,
        out_shape=(
            shape(8, 64, 512),
            shape(8, 64, 512),
            shape(8, 64, 256),
            shape(8, 4, 64, 256),
            shape(2, 16, 256, dtype=F32),
        ),
        in_specs=[SMEM_SPEC] + vmem(5),
        out_specs=tuple(vmem(5)),
        scratch_shapes=[
            pltpu.VMEM((4, 64, 256), BF16),
            pltpu.VMEM((32, 64, 256), BF16),
            pltpu.VMEM((8, 4, 64, 256), BF16),
            DMA((3, 8)),
            DMA((3, 8)),
            DMA((2,)),
            DMA((2,)),
            DMA((4,)),
            DMA((4,)),
            DMA((2, 4, 2)),
            DMA((2, 4, 2)),
            DMA((8,)),
            DMA((8,)),
            DMA((2,)),
        ],
        compiler_params=pltpu.CompilerParams(
            collective_id=0, has_side_effects=True, vmem_limit_bytes=VMEM_LIMIT
        ),
        name="gather",
    )(tab, queries, out_grad, keys, values, ld)

    dq, own_part, gate_part = pl.pallas_call(
        attend_kernel,
        out_shape=(shape(8, 64, 512), shape(8, 64, 256), shape(8, 4, 64, 256)),
        in_specs=[SMEM_SPEC] + vmem(5),
        out_specs=tuple(vmem(3)),
        compiler_params=pltpu.CompilerParams(vmem_limit_bytes=VMEM_LIMIT),
        name="attend",
    )(tab, q_in, o_in, own_kv, gkv, ld_in)

    return pl.pallas_call(
        scatter_kernel,
        out_shape=(shape(64, 4096), shape(64, 512), shape(64, 512)),
        in_specs=[SMEM_SPEC] + vmem(3),
        out_specs=tuple(vmem(3)),
        scratch_shapes=[
            pltpu.VMEM((8, 64, 256), BF16),
            pltpu.VMEM((8, 4, 64, 256), BF16),
            pltpu.VMEM((33, 64, 256), F32),
            pltpu.VMEM((2, 4, 2, 2, 64, 256), BF16),
            pltpu.VMEM((2, 4, 2, 2, 64, 256), BF16),
            pltpu.VMEM((4, 64, 256), BF16),
            pltpu.VMEM((4, 64, 256), BF16),
            DMA((2, 8)),
            DMA((2, 8)),
            DMA((8,)),
            DMA((8,)),
            DMA((2, 4, 2)),
            DMA((2, 4, 2)),
            DMA((4,)),
            DMA((4,)),
            DMA(()),
        ],
        compiler_params=pltpu.CompilerParams(
            collective_id=1, has_side_effects=True, vmem_limit_bytes=VMEM_LIMIT
        ),
        name="scatter",
    )(tab, dq, own_part, gate_part)


def solution(mesh):
    rows = P(("ctx", "head"), None)
    return jax.shard_map(
        shards,
        mesh=mesh,
        in_specs=(rows, rows, rows, rows, P("ctx", "head"), P("ctx", "head"), P()),
        out_specs=(rows, rows, rows),
        check_vma=False,
    )
```

```python
import math

import jax
import jax.numpy as jnp
from jax import lax
from jax.experimental import pallas as pl
from jax.experimental.pallas import tpu as pltpu
from jax.sharding import PartitionSpec as P

MESH = pl.DeviceIdType.MESH
LOG2E = math.log2(math.e)
SCALE = 1.0 / math.sqrt(128.0)
F32 = jnp.float32
BF16 = jnp.bfloat16
PARTS = 2
PART = 64 // PARTS


def flip(bit, by):
    return bit if by == 0 else 1 - bit


def xor(a, b):
    return lax.rem(a + b, 2)


class Place:
    def __init__(self):
        ctx, head = lax.axis_index("ctx"), lax.axis_index("head")
        self.z = ctx // 8
        self.X = lax.rem(ctx // 4, 2)
        self.Y = lax.rem(ctx // 2, 2)
        self.yl = lax.rem(ctx, 2)
        self.xl = head // 2
        self.c = lax.rem(head, 2)
        self.gx, self.gy = xor(self.xl, self.X), xor(self.yl, self.Y)
        self.g = self.gx * 2 + self.gy
        self.e = self.g * 2 + self.c
        self.s = self.yl * 4 + self.xl * 2 + self.c
        self.m = self.X * 4 + self.Y * 2 + self.c
        self.b = self.z * 4 + self.X * 2 + self.Y

    def inner(self, k):
        yl, xl, c = flip(self.yl, k // 4), flip(self.xl, k // 2 % 2), flip(self.c, k % 2)
        e = (xor(xl, self.X) * 2 + xor(yl, self.Y)) * 2 + c
        return device(self.z, self.X, xl, self.Y, yl, c), yl * 4 + xl * 2 + c, e

    def row(self, k):
        X, Y, c = flip(self.X, k // 4), flip(self.Y, k // 2 % 2), flip(self.c, k % 2)
        return device(self.z, X, xor(self.gx, X), Y, xor(self.gy, Y), c), X * 4 + Y * 2 + c

    def plane(self, step):
        return lax.rem(self.z + step, 8)

    def taker(self, d, g):
        return device(d, self.xl, xor(self.xl, g // 2), self.yl, xor(self.yl, g % 2), self.c)

    def owner(self, d, w):
        return device(d, w // 2, self.X, w % 2, self.Y, self.c)

    def above(self):
        return {"ctx": lax.rem(self.z + 1, 8) * 8 + self.X * 4 + self.Y * 2 + self.yl}

    def below(self):
        return {"ctx": lax.rem(self.z + 7, 8) * 8 + self.X * 4 + self.Y * 2 + self.yl}

    def barrier_signal(self, sem):
        for k in range(1, 32):
            to = device(
                self.z,
                flip(self.X, k // 16),
                flip(self.xl, k // 8 % 2),
                flip(self.Y, k // 4 % 2),
                flip(self.yl, k // 2 % 2),
                flip(self.c, k % 2),
            )
            pl.semaphore_signal(sem, inc=1, device_id=to, device_id_type=MESH)
        for to in (self.above(), self.below()):
            pl.semaphore_signal(sem, inc=1, device_id=to, device_id_type=MESH)
        for d in (self.plane(1), self.plane(7)):
            for i in range(4):
                pl.semaphore_signal(sem, inc=1, device_id=self.taker(d, i), device_id_type=MESH)
            for i in range(1, 4):
                X, Y = flip(self.xl, i // 2), flip(self.yl, i % 2)
                to = device(d, X, self.X, Y, self.Y, self.c)
                pl.semaphore_signal(sem, inc=1, device_id=to, device_id_type=MESH)


BARRIER_COUNT = 47


def device(z, X, xl, Y, yl, c):
    return {"ctx": z * 8 + X * 4 + Y * 2 + yl, "head": xl * 2 + c}


def remote(src, dst, send, recv, to):
    return pltpu.make_async_remote_copy(
        src_ref=src, dst_ref=dst, send_sem=send, recv_sem=recv, device_id=to, device_id_type=MESH
    )


def dot(a, b, contract):
    return lax.dot_general(a, b, ((contract[:1], contract[1:]), ((), ())), preferred_element_type=F32)


def terms(q, o, lse, delta, k, v, mask):
    scores = dot(k, q, (1, 1)) * (SCALE * LOG2E)
    weights = jnp.exp2(scores - lse)
    if mask is not None:
        weights = jnp.where(mask, weights, 0.0)
    slopes = weights * (dot(v, o, (1, 1)) - delta)
    return weights.astype(BF16), slopes.astype(BF16)


def kernel(
    tab,
    q_ref,
    o_ref,
    k_ref,
    v_ref,
    ld_ref,
    out_q,
    out_k,
    out_v,
    q_in,
    o_in,
    own_kv,
    ld_in,
    kvl,
    kvz_0,
    kvz_1,
    picked,
    gkv,
    gate_out,
    gate_in,
    own_out,
    own_in,
    dq_sum,
    dq_out,
    run,
    z_out,
    z_in,
    end_out,
    end_in,
    q_send,
    q_recv,
    ld_send,
    ld_recv,
    n_send,
    n_recv,
    z_send,
    z_recv,
    r_send,
    r_recv,
    b_send,
    b_recv,
    g_send,
    g_recv,
    s_send,
    s_recv,
    e_send,
    e_recv,
    l_sem,
):
    kvz = (kvz_0, kvz_1)
    me = Place()
    barrier = pltpu.get_barrier_semaphore()
    me.barrier_signal(barrier)
    for g in range(4):
        kvl[g, :, :128] = k_ref[:, g * 128 : (g + 1) * 128]
        kvl[g, :, 128:] = v_ref[:, g * 128 : (g + 1) * 128]
    for i in range(PARTS):
        run[i, 32] = jnp.zeros((PART, 256), F32)
    pl.semaphore_wait(barrier, BARRIER_COUNT)

    staying = (me.xl == me.X) & (me.yl == me.Y)
    sent = []
    maybe_sent = []

    def start(copy, here=None, local=None):
        if here is None:
            copy.start()
            sent.append(copy)
            return

        @pl.when(here)
        def _():
            local()

        @pl.when(jnp.logical_not(here))
        def _():
            copy.start()

        maybe_sent.append((here, copy))

    def await_part(part, send, recv, here=None):
        copy = remote(part, part, send, recv, me.above())
        if here is None:
            copy.wait_recv()
            return

        @pl.when(jnp.logical_not(here))
        def _():
            copy.wait_recv()

    slot = me.X * 2 + me.Y
    for i in range(PARTS):
        for n, step in enumerate((1, 7, 0)):
            for g in range(4):
                copy = remote(
                    kvl.at[g, pl.ds(i * PART, PART)],
                    kvz[i].at[me.b],
                    n_send.at[n, g, i],
                    n_recv.at[n, slot, i],
                    me.taker(me.plane(step), g),
                )
                if n == 2 and g == 0:

                    def keep():
                        kvz[i][me.b] = kvl[0, i * PART : (i + 1) * PART]

                    start(copy, staying, keep)
                else:
                    start(copy)

    for k in range(1, 8):
        to, _, e = me.inner(k)
        start(remote(kvl.at[e // 2], own_kv.at[me.s], q_send.at[2, k], q_recv.at[2, k], to))
    ld_yl = xor(me.c, me.Y)
    ld_xl = xor(me.xl, me.X)
    for core in range(2):
        to = device(me.z, me.X, ld_xl, me.Y, ld_yl, core)
        here = (ld_xl == me.xl) & (ld_yl == me.yl) & (me.c == core)

        def keep():
            ld_in[me.yl] = ld_ref[...]

        start(
            remote(ld_ref, ld_in.at[me.yl], ld_send.at[core], ld_recv.at[me.yl], to), here, keep
        )
    for k in range(1, 8):
        to, _, e = me.inner(k)
        cols = pl.ds(pl.multiple_of(e * 512, 512), 512)
        for i, (src, dst) in enumerate(((q_ref, q_in), (o_ref, o_in))):
            start(remote(src.at[:, cols], dst.at[me.s], q_send.at[i, k], q_recv.at[i, k], to))
    my_cols = pl.ds(pl.multiple_of(me.e * 512, 512), 512)
    local = [
        pltpu.make_async_copy(src.at[:, my_cols], dst.at[me.s], l_sem.at[i])
        for i, (src, dst) in enumerate(((q_ref, q_in), (o_ref, o_in)))
    ]
    for copy in local:
        copy.start()
    own_kv[me.s] = kvl[me.g]

    neighbour = (me.above(), me.below())

    def chunk(d, i, first, count):
        return kvz[i].at[pl.ds(lax.rem(d + 8, 8) * 4 + first, count)]

    def pass_on(way, t, i):
        d = me.z - t if way == 0 else me.z + t
        part = chunk(d, i, *((way * 2, 2) if t == 3 else (0, 4)))
        start(remote(part, part, z_send.at[way, t, i], z_recv.at[way, t, i], neighbour[way]))

    def arrived(way, t, i):
        d = me.z - t - 1 if way == 0 else me.z + t + 1
        part = chunk(d, i, *((way * 2, 2) if t == 3 else (0, 4)))
        await_part(part, z_send.at[way, t, i], z_recv.at[way, t, i])

    def arrived_first(n, i):
        d = (me.z + 7, me.z + 1, me.z)[n]
        for w in range(4):
            block = kvz[i].at[lax.rem(d, 8) * 4 + w]
            here = staying & (slot == w) if n == 2 else None
            await_part(block, n_send.at[n, 0, i], n_recv.at[n, w, i], here)

    for i in range(PARTS):
        for way in range(2):
            arrived_first(way, i)
            pass_on(way, 1, i)

    def pick(i):
        for k in (7, 6, 5, 4, 3, 2, 1, 0):
            to, p = me.row(k)
            for h in range(4):
                got = kvz[i][tab[0, p * 4 + h]]
                if k == 0:
                    gkv[i, me.m, h] = got
                else:
                    picked[i, k, h] = got
            if k:
                start(
                    remote(picked.at[i, k], gkv.at[i, me.m], r_send.at[i, k], r_recv.at[i, k], to)
                )

    for t in range(2, 4):
        for i in range(PARTS):
            for way in range(2):
                arrived(way, t - 1, i)
                pass_on(way, t, i)
    for i in range(PARTS):
        for way in range(2):
            arrived(way, 3, i)
        arrived_first(2, i)
        pick(i)

    for copy in local:
        copy.wait()
    for k in range(1, 8):
        _, s, _ = me.inner(k)
        for i, dst in enumerate((q_in, o_in, own_kv)):
            await_part(dst.at[s], q_send.at[i, k], q_recv.at[i, k])
    for yl in range(2):
        here = (me.gx == me.xl) & (me.gy == me.c) & (me.yl == yl)
        await_part(ld_in.at[yl], ld_send.at[0], ld_recv.at[yl], here)

    def rows_of(h):
        row = 4 * me.c + h
        lse = jnp.concatenate([ld_in[i, pl.ds(row, 1), :] for i in range(2)], axis=1) * LOG2E
        delta = jnp.concatenate([ld_in[i, pl.ds(row + 8, 1), :] for i in range(2)], axis=1)
        lanes = slice(h * 128, (h + 1) * 128)
        q = q_in[:, :, lanes].reshape(512, 128)
        o = o_in[:, :, lanes].reshape(512, 128)
        return q, o, lse, delta

    TILE = 256
    key_pos = lax.broadcasted_iota(jnp.int32, (TILE, TILE), 0)
    query_pos = lax.broadcasted_iota(jnp.int32, (TILE, TILE), 1)
    causal = key_pos <= query_pos
    own = own_kv[...].reshape(512, 256)
    own_k, own_v = own[:, :128], own[:, 128:]
    own_dk = [jnp.zeros((TILE, 128), F32) for _ in range(2)]
    own_dv = [jnp.zeros((TILE, 128), F32) for _ in range(2)]
    for h in range(4):
        q, o, lse, delta = rows_of(h)
        for i in range(2):
            cols = slice(i * TILE, (i + 1) * TILE)
            dq = jnp.zeros((TILE, 128), F32)
            for j in range(i + 1):
                keys = slice(j * TILE, (j + 1) * TILE)
                mask = causal if i == j else None
                w, s = terms(
                    q[cols], o[cols], lse[:, cols], delta[:, cols], own_k[keys], own_v[keys], mask
                )
                own_dv[j] += dot(w, o[cols], (1, 0))
                own_dk[j] += dot(s, q[cols], (1, 0))
                dq += dot(s, own_k[keys], (0, 0))
            dq_sum[h, cols] = dq
    for j in range(2):
        part = jnp.concatenate([own_dk[j] * SCALE, own_dv[j]], axis=1).astype(BF16)
        own_out[j * 4 : (j + 1) * 4] = part.reshape(4, 64, 256)
    for k in range(1, 8):
        to, s, _ = me.inner(k)
        start(remote(own_out.at[s], own_in.at[me.e], q_send.at[3, k], q_recv.at[3, k], to))
    own_in[me.e] = own_out[me.s]

    keys = 8 * PART
    for i in range(PARTS):
        for k in range(1, 8):
            _, p = me.row(k)
            await_part(gkv.at[i, p], r_send.at[i, k], r_recv.at[i, k])
        for h in range(4):
            q, o, lse, delta = rows_of(h)
            lse = jnp.where(tab[0, me.m * 4 + h] != me.b, lse, 1e30)
            kv = gkv[i, :, h].reshape(keys, 256)
            k_rows, v_rows = kv[:, :128], kv[:, 128:]
            dk = jnp.zeros((keys, 128), F32)
            dv = jnp.zeros((keys, 128), F32)
            for j in range(2):
                cols = slice(j * TILE, (j + 1) * TILE)
                w, s = terms(q[cols], o[cols], lse[:, cols], delta[:, cols], k_rows, v_rows, None)
                dv += dot(w, o[cols], (1, 0))
                dk += dot(s, q[cols], (1, 0))
                dq = dq_sum[h, cols] + dot(s, k_rows, (0, 0))
                if i < PARTS - 1:
                    dq_sum[h, cols] = dq
                else:
                    part = (dq * SCALE).astype(BF16).reshape(4, 64, 128)
                    dq_out[j * 4 : (j + 1) * 4, :, h * 128 : (h + 1) * 128] = part
            part = jnp.concatenate([dk * SCALE, dv], axis=1).astype(BF16)
            gate_out[i, :, h] = part.reshape(8, PART, 256)
        for k in (7, 6, 5, 4, 3, 2, 1):
            to, p = me.row(k)
            start(
                remote(gate_out.at[i, p], gate_in.at[i, me.m], b_send.at[i, k], b_recv.at[i, k], to)
            )
        gate_in[i, me.m] = gate_out[i, me.m]
    for k in range(1, 8):
        to, s, _ = me.inner(k)
        start(remote(dq_out.at[s], out_q.at[:, my_cols], g_send.at[k], g_recv.at[k], to))
    dq_local = pltpu.make_async_copy(dq_out.at[me.s], out_q.at[:, my_cols], l_sem.at[0])
    dq_local.start()

    def add_up(i):
        for k in range(1, 8):
            _, p = me.row(k)
            await_part(gate_in.at[i, p], b_send.at[i, k], b_recv.at[i, k])

        def add(j, carry):
            run[i, j] = gate_in[i, j // 4, lax.rem(j, 4)].astype(F32) + run[i, tab[1, j]]
            return carry

        lax.fori_loop(0, 32, add, 0)

    def total(i, d, w):
        return run[i, tab[2, lax.rem(d + 8, 8) * 4 + w]]

    def sum_on(way, t, i):
        d = me.z + 4 - t if way == 0 else me.z - 4 + t
        first = way * 2
        if t:
            part = z_in.at[way, t - 1, i]
            if t == 1:
                part = part.at[pl.ds(first, 2)]
            await_part(part, s_send.at[way, t - 1, i], s_recv.at[way, t - 1, i])
        for w in range(4):
            half = first <= w < first + 2
            if t == 0 and not half:
                continue
            value = total(i, d, w)
            if t >= 2 or (t == 1 and half):
                value += z_in[way, t - 1, i, w].astype(F32)
            z_out[way, t, i, w] = value.astype(BF16)
        if t < 3:
            src, dst = z_out.at[way, t, i], z_in.at[way, t, i]
            if t == 0:
                src, dst = src.at[pl.ds(first, 2)], dst.at[pl.ds(first, 2)]
            start(remote(src, dst, s_send.at[way, t, i], s_recv.at[way, t, i], neighbour[way]))
        else:
            for w in range(4):
                start(
                    remote(
                        z_out.at[way, t, i, w],
                        end_in.at[way, me.g, i],
                        e_send.at[way, w, i],
                        e_recv.at[way, me.g, i],
                        me.owner(lax.rem(d + 8, 8), w),
                    )
                )

    def sum_here(i):
        for w in range(4):
            end_out[i, w] = total(i, me.z, w).astype(BF16)
            copy = remote(
                end_out.at[i, w],
                end_in.at[2, me.g, i],
                e_send.at[2, w, i],
                e_recv.at[2, me.g, i],
                me.owner(me.z, w),
            )

            def keep():
                end_in[2, 0, i] = end_out[i, w]

            start(copy, staying & (slot == w), keep)

    add_up(0)
    for t in range(2):
        for way in range(2):
            sum_on(way, t, 0)
    for i in range(1, PARTS):
        add_up(i)
        for way in range(2):
            sum_on(way, 0, i)
    for t in range(1, 4):
        for i in range(PARTS):
            if i == 0 and t == 1:
                continue
            for way in range(2):
                sum_on(way, t, i)
    for i in range(PARTS):
        sum_here(i)

    for k in range(1, 8):
        _, _, e = me.inner(k)
        await_part(own_in.at[e], q_send.at[3, k], q_recv.at[3, k])
    for i in range(PARTS):
        toks = slice(i * PART, (i + 1) * PART)
        for g in range(4):
            value = own_in[2 * g, toks].astype(F32) + own_in[2 * g + 1, toks].astype(F32)
            for n in range(3):
                here = staying if n == 2 and g == 0 else None
                await_part(end_in.at[n, g, i], e_send.at[n, g, i], e_recv.at[n, g, i], here)
                value += end_in[n, g, i].astype(F32)
            out_k[toks, g * 128 : (g + 1) * 128] = value[:, :128].astype(BF16)
            out_v[toks, g * 128 : (g + 1) * 128] = value[:, 128:].astype(BF16)

    dq_local.wait()
    for k in range(1, 8):
        _, _, e = me.inner(k)
        part = out_q.at[:, pl.ds(pl.multiple_of(e * 512, 512), 512)]
        await_part(part, g_send.at[k], g_recv.at[k])
    for here, copy in maybe_sent:

        @pl.when(jnp.logical_not(here))
        def _():
            copy.wait_send()

    for copy in sent:
        copy.wait_send()


def vmem(count):
    return [pl.BlockSpec(memory_space=pltpu.VMEM)] * count


SMEM_SPEC = pl.BlockSpec(memory_space=pltpu.SMEM)
ANY_SPEC = pl.BlockSpec(memory_space=pl.ANY)
DMA = pltpu.SemaphoreType.DMA
VMEM_LIMIT = 48 * 1024 * 1024


def shape(*dims, dtype=BF16):
    return jax.ShapeDtypeStruct(dims, dtype)


def shards(queries, keys, values, out_grad, lse, delta, gate_block):
    ctx, head = lax.axis_index("ctx"), lax.axis_index("head")
    z, X, Y, yl, xl = ctx // 8, ctx // 4 % 2, ctx // 2 % 2, ctx % 2, head // 2
    g = (xl + X) % 2 * 2 + (yl + Y) % 2
    gates = lax.dynamic_slice(gate_block, (z * 4, g * 8), (4, 8)).reshape(32)
    slots = jnp.arange(32, dtype=jnp.int32)
    same = (gates[:, None] == gates[None, :]) & (slots[None, :] < slots[:, None])
    previous = jnp.max(jnp.where(same, slots[None, :], -1), axis=1)
    member = gates[None, :] == slots[:, None]
    last = jnp.max(jnp.where(member, slots[None, :], -1), axis=1)
    tab = jnp.stack([gates, jnp.where(previous < 0, 32, previous), jnp.where(last < 0, 32, last)])
    ld = jnp.concatenate([lse.T, delta.T], axis=0)

    def buf(*dims, dtype=BF16):
        return pltpu.VMEM(dims, dtype)

    return pl.pallas_call(
        kernel,
        out_shape=(shape(64, 4096), shape(64, 512), shape(64, 512)),
        in_specs=[SMEM_SPEC, ANY_SPEC, ANY_SPEC] + vmem(3),
        out_specs=(ANY_SPEC, *vmem(2)),
        scratch_shapes=[
            buf(8, 64, 512),
            buf(8, 64, 512),
            buf(8, 64, 256),
            buf(2, 16, 256, dtype=F32),
            buf(4, 64, 256),
            buf(32, PART, 256),
            buf(32, PART, 256),
            buf(PARTS, 8, 4, PART, 256),
            buf(PARTS, 8, 4, PART, 256),
            buf(PARTS, 8, 4, PART, 256),
            buf(PARTS, 8, 4, PART, 256),
            buf(8, 64, 256),
            buf(8, 64, 256),
            buf(4, 512, 128, dtype=F32),
            buf(8, 64, 512),
            buf(PARTS, 33, PART, 256, dtype=F32),
            buf(2, 4, PARTS, 4, PART, 256),
            buf(2, 4, PARTS, 4, PART, 256),
            buf(PARTS, 4, PART, 256),
            buf(3, 4, PARTS, PART, 256),
            DMA((4, 8)),
            DMA((4, 8)),
            DMA((2,)),
            DMA((2,)),
            DMA((3, 4, PARTS)),
            DMA((3, 4, PARTS)),
            DMA((2, 4, PARTS)),
            DMA((2, 4, PARTS)),
            DMA((PARTS, 8)),
            DMA((PARTS, 8)),
            DMA((PARTS, 8)),
            DMA((PARTS, 8)),
            DMA((8,)),
            DMA((8,)),
            DMA((2, 4, PARTS)),
            DMA((2, 4, PARTS)),
            DMA((3, 4, PARTS)),
            DMA((3, 4, PARTS)),
            DMA((2,)),
        ],
        compiler_params=pltpu.CompilerParams(
            collective_id=0, has_side_effects=True, vmem_limit_bytes=VMEM_LIMIT
        ),
        name="block_attention_backward",
    )(tab, queries, out_grad, keys, values, ld)


def solution(mesh):
    rows = P(("ctx", "head"), None)
    return jax.shard_map(
        shards,
        mesh=mesh,
        in_specs=(rows, rows, rows, rows, P("ctx", "head"), P("ctx", "head"), P()),
        out_specs=(rows, rows, rows),
        check_vma=False,
    )
```

```python
import math

import jax
import jax.numpy as jnp
from jax import lax
from jax.experimental import pallas as pl
from jax.experimental.pallas import tpu as pltpu
from jax.sharding import PartitionSpec as P

MESH = pl.DeviceIdType.MESH
LOG2E = math.log2(math.e)
SCALE = 1.0 / math.sqrt(128.0)
F32 = jnp.float32
BF16 = jnp.bfloat16
PARTS = 4
PART = 64 // PARTS


def flip(bit, by):
    return bit if by == 0 else 1 - bit


def xor(a, b):
    return lax.rem(a + b, 2)


class Place:
    def __init__(self):
        ctx, head = lax.axis_index("ctx"), lax.axis_index("head")
        self.z = ctx // 8
        self.X = lax.rem(ctx // 4, 2)
        self.Y = lax.rem(ctx // 2, 2)
        self.yl = lax.rem(ctx, 2)
        self.xl = head // 2
        self.c = lax.rem(head, 2)
        self.gx, self.gy = xor(self.xl, self.X), xor(self.yl, self.Y)
        self.g = self.gx * 2 + self.gy
        self.e = self.g * 2 + self.c
        self.s = self.yl * 4 + self.xl * 2 + self.c
        self.m = self.X * 4 + self.Y * 2 + self.c
        self.b = self.z * 4 + self.X * 2 + self.Y

    def inner(self, k):
        yl, xl, c = flip(self.yl, k // 4), flip(self.xl, k // 2 % 2), flip(self.c, k % 2)
        e = (xor(xl, self.X) * 2 + xor(yl, self.Y)) * 2 + c
        return device(self.z, self.X, xl, self.Y, yl, c), yl * 4 + xl * 2 + c, e

    def row(self, k):
        X, Y, c = flip(self.X, k // 4), flip(self.Y, k // 2 % 2), flip(self.c, k % 2)
        return device(self.z, X, xor(self.gx, X), Y, xor(self.gy, Y), c), X * 4 + Y * 2 + c

    def taker(self, step, g):
        z = lax.rem(self.z + step + 8, 8)
        return device(z, self.xl, xor(self.xl, g // 2), self.yl, xor(self.yl, g % 2), self.c)

    def owner(self, w):
        return device(self.z, w // 2, self.X, w % 2, self.Y, self.c)

    def plane(self, step):
        return {"ctx": lax.rem(self.z + step + 8, 8) * 8 + self.X * 4 + self.Y * 2 + self.yl}

    def barrier_signal(self, sem):
        for k in range(1, 32):
            to = device(
                self.z,
                flip(self.X, k // 16),
                flip(self.xl, k // 8 % 2),
                flip(self.Y, k // 4 % 2),
                flip(self.yl, k // 2 % 2),
                flip(self.c, k % 2),
            )
            pl.semaphore_signal(sem, inc=1, device_id=to, device_id_type=MESH)
        for step in (1, -1, 2, -2):
            pl.semaphore_signal(sem, inc=1, device_id=self.plane(step), device_id_type=MESH)
        for step in (1, -1):
            for i in range(4):
                to = self.taker(step, i)
                pl.semaphore_signal(sem, inc=1, device_id=to, device_id_type=MESH)
            for i in range(1, 4):
                X, Y = flip(self.xl, i // 2), flip(self.yl, i % 2)
                to = device(lax.rem(self.z + step + 8, 8), X, self.X, Y, self.Y, self.c)
                pl.semaphore_signal(sem, inc=1, device_id=to, device_id_type=MESH)


BARRIER_COUNT = 49


def device(z, X, xl, Y, yl, c):
    return {"ctx": z * 8 + X * 4 + Y * 2 + yl, "head": xl * 2 + c}


def remote(src, dst, send, recv, to):
    return pltpu.make_async_remote_copy(
        src_ref=src, dst_ref=dst, send_sem=send, recv_sem=recv, device_id=to, device_id_type=MESH
    )


def dot(a, b, contract):
    return lax.dot_general(a, b, ((contract[:1], contract[1:]), ((), ())), preferred_element_type=F32)


def terms(q, o, lse, delta, k, v, mask):
    scores = dot(k, q, (1, 1)) * (SCALE * LOG2E)
    weights = jnp.exp2(scores - lse)
    if mask is not None:
        weights = jnp.where(mask, weights, 0.0)
    slopes = weights * (dot(v, o, (1, 1)) - delta)
    return weights.astype(BF16), slopes.astype(BF16)


def kernel(
    gate_ref,
    q_ref,
    o_ref,
    k_ref,
    v_ref,
    l_ref,
    d_ref,
    out_q,
    out_k,
    out_v,
    tab,
    ld_ref,
    q_in,
    o_in,
    own_kv,
    ld_in,
    kvl,
    kvz_0,
    kvz_1,
    kvz_2,
    kvz_3,
    picked,
    gkv,
    gate_out,
    gate_in,
    own_out,
    own_in,
    dq_sum,
    dq_out,
    run,
    z_out,
    z_in,
    end_out,
    end_in,
    q_send,
    q_recv,
    ld_send,
    ld_recv,
    n_send,
    n_recv,
    z_send,
    z_recv,
    r_send,
    r_recv,
    b_send,
    b_recv,
    g_send,
    g_recv,
    s_send,
    s_recv,
    e_send,
    e_recv,
    l_sem,
):
    kvz = (kvz_0, kvz_1, kvz_2, kvz_3)
    me = Place()
    barrier = pltpu.get_barrier_semaphore()
    me.barrier_signal(barrier)
    for g in range(4):
        kvl[g, :, :128] = k_ref[:, g * 128 : (g + 1) * 128]
        kvl[g, :, 128:] = v_ref[:, g * 128 : (g + 1) * 128]
    ld_ref[:8], ld_ref[8:] = l_ref[...], d_ref[...]
    for i in range(PARTS):
        run[i, 32] = jnp.zeros((PART, 256), F32)
    pl.semaphore_wait(barrier, BARRIER_COUNT)

    staying = (me.xl == me.X) & (me.yl == me.Y)
    sent = []
    maybe_sent = []

    def start(copy, here=None, local=None):
        if here is None:
            copy.start()
            sent.append(copy)
            return

        @pl.when(here)
        def _():
            local()

        @pl.when(jnp.logical_not(here))
        def _():
            copy.start()

        maybe_sent.append((here, copy))

    def await_part(part, send, recv, here=None):
        copy = remote(part, part, send, recv, me.plane(1))
        if here is None:
            copy.wait_recv()
            return

        @pl.when(jnp.logical_not(here))
        def _():
            copy.wait_recv()

    slot = me.X * 2 + me.Y
    STEPS = (1, -1, 0)
    for i in range(PARTS):
        for n, step in enumerate(STEPS):
            for g in range(4):
                copy = remote(
                    kvl.at[g, pl.ds(i * PART, PART)],
                    kvz[i].at[me.b],
                    n_send.at[n, g, i],
                    n_recv.at[n, slot, i],
                    me.taker(step, g),
                )
                if step == 0 and g == 0:

                    def keep():
                        kvz[i][me.b] = kvl[0, i * PART : (i + 1) * PART]

                    start(copy, staying, keep)
                else:
                    start(copy)

    for k in range(1, 8):
        to, _, e = me.inner(k)
        start(remote(kvl.at[e // 2], own_kv.at[me.s], q_send.at[2, k], q_recv.at[2, k], to))
    ld_yl = xor(me.c, me.Y)
    ld_xl = xor(me.xl, me.X)
    for core in range(2):
        to = device(me.z, me.X, ld_xl, me.Y, ld_yl, core)
        here = (ld_xl == me.xl) & (ld_yl == me.yl) & (me.c == core)

        def keep():
            ld_in[me.yl] = ld_ref[...]

        start(
            remote(ld_ref, ld_in.at[me.yl], ld_send.at[core], ld_recv.at[me.yl], to), here, keep
        )
    for k in range(1, 8):
        to, _, e = me.inner(k)
        cols = pl.ds(pl.multiple_of(e * 512, 512), 512)
        for i, (src, dst) in enumerate(((q_ref, q_in), (o_ref, o_in))):
            start(remote(src.at[:, cols], dst.at[me.s], q_send.at[i, k], q_recv.at[i, k], to))
    my_cols = pl.ds(pl.multiple_of(me.e * 512, 512), 512)
    local = [
        pltpu.make_async_copy(src.at[:, my_cols], dst.at[me.s], l_sem.at[i])
        for i, (src, dst) in enumerate(((q_ref, q_in), (o_ref, o_in)))
    ]
    for copy in local:
        copy.start()
    own_kv[me.s] = kvl[me.g]

    def fill(j, carry):
        tab[0, j] = gate_ref[me.z * 4 + j // 8, me.g * 8 + lax.rem(j, 8)]
        return carry

    def link(j, carry):
        mine = tab[0, j]
        previous, last = jnp.int32(32), jnp.int32(32)
        for other in range(32):
            gate = tab[0, other]
            previous = jnp.where((gate == mine) & (other < j), other, previous)
            last = jnp.where(gate == j, other, last)
        tab[1, j] = previous
        tab[2, j] = last
        return carry

    lax.fori_loop(0, 32, fill, 0)
    lax.fori_loop(0, 32, link, 0)

    def chunk(d, i, first, count):
        return kvz[i].at[pl.ds(lax.rem(d + 8, 8) * 4 + first, count)]

    def span(way, t):
        return (way * 2, 2) if t == 3 else (0, 4)

    def pass_on(way, t, i):
        sign = 1 - 2 * way
        part = chunk(me.z - sign * t, i, *span(way, t))
        start(remote(part, part, z_send.at[way, t, i], z_recv.at[way, t, i], me.plane(sign)))

    def arrived(way, t, i):
        part = chunk(me.z - (1 - 2 * way) * (t + 1), i, *span(way, t))
        await_part(part, z_send.at[way, t, i], z_recv.at[way, t, i])

    def arrived_first(n, i):
        for w in range(4):
            block = kvz[i].at[lax.rem(me.z - STEPS[n] + 8, 8) * 4 + w]
            here = staying & (slot == w) if n == 2 else None
            await_part(block, n_send.at[n, 0, i], n_recv.at[n, w, i], here)

    def pick(i):
        for k in (7, 6, 5, 4, 3, 2, 1, 0):
            to, p = me.row(k)
            for h in range(4):
                got = kvz[i][tab[0, p * 4 + h]]
                if k == 0:
                    gkv[i, me.m, h] = got
                else:
                    picked[i, k, h] = got
            if k:
                start(
                    remote(picked.at[i, k], gkv.at[i, me.m], r_send.at[i, k], r_recv.at[i, k], to)
                )

    def both(what, *args):
        for way in range(2):
            what(*args[:-2], way, *args[-2:])

    for i in range(PARTS):
        for way in range(2):
            arrived_first(way, i)
            pass_on(way, 1, i)
    for t in (2, 3):
        for i in range(PARTS):
            for way in range(2):
                arrived(way, t - 1, i)
                pass_on(way, t, i)
    for i in range(PARTS):
        both(arrived, 3, i)
        arrived_first(2, i)
        pick(i)

    for copy in local:
        copy.wait()
    for k in range(1, 8):
        _, s, _ = me.inner(k)
        for i, dst in enumerate((q_in, o_in, own_kv)):
            await_part(dst.at[s], q_send.at[i, k], q_recv.at[i, k])
    for yl in range(2):
        here = (me.gx == me.xl) & (me.gy == me.c) & (me.yl == yl)
        await_part(ld_in.at[yl], ld_send.at[0], ld_recv.at[yl], here)

    def rows_of(h):
        row = 4 * me.c + h
        lse = jnp.concatenate([ld_in[i, pl.ds(row, 1), :] for i in range(2)], axis=1) * LOG2E
        delta = jnp.concatenate([ld_in[i, pl.ds(row + 8, 1), :] for i in range(2)], axis=1)
        lanes = slice(h * 128, (h + 1) * 128)
        q = q_in[:, :, lanes].reshape(512, 128)
        o = o_in[:, :, lanes].reshape(512, 128)
        return q, o, lse, delta

    TILE = 256
    key_pos = lax.broadcasted_iota(jnp.int32, (TILE, TILE), 0)
    query_pos = lax.broadcasted_iota(jnp.int32, (TILE, TILE), 1)
    causal = key_pos <= query_pos
    own = own_kv[...].reshape(512, 256)
    own_k, own_v = own[:, :128], own[:, 128:]
    own_dk = [jnp.zeros((TILE, 128), F32) for _ in range(2)]
    own_dv = [jnp.zeros((TILE, 128), F32) for _ in range(2)]
    for h in range(4):
        q, o, lse, delta = rows_of(h)
        for i in range(2):
            cols = slice(i * TILE, (i + 1) * TILE)
            dq = jnp.zeros((TILE, 128), F32)
            for j in range(i + 1):
                keys = slice(j * TILE, (j + 1) * TILE)
                mask = causal if i == j else None
                w, s = terms(
                    q[cols], o[cols], lse[:, cols], delta[:, cols], own_k[keys], own_v[keys], mask
                )
                own_dv[j] += dot(w, o[cols], (1, 0))
                own_dk[j] += dot(s, q[cols], (1, 0))
                dq += dot(s, own_k[keys], (0, 0))
            dq_sum[h, cols] = dq
    for j in range(2):
        part = jnp.concatenate([own_dk[j] * SCALE, own_dv[j]], axis=1).astype(BF16)
        own_out[j * 4 : (j + 1) * 4] = part.reshape(4, 64, 256)
    for k in range(1, 8):
        to, s, _ = me.inner(k)
        start(remote(own_out.at[s], own_in.at[me.e], q_send.at[3, k], q_recv.at[3, k], to))
    own_in[me.e] = own_out[me.s]

    keys = 8 * PART
    for i in range(PARTS):
        for k in range(1, 8):
            _, p = me.row(k)
            await_part(gkv.at[i, p], r_send.at[i, k], r_recv.at[i, k])
        for h in range(4):
            q, o, lse, delta = rows_of(h)
            lse = jnp.where(tab[0, me.m * 4 + h] != me.b, lse, 1e30)
            kv = gkv[i, :, h].reshape(keys, 256)
            k_rows, v_rows = kv[:, :128], kv[:, 128:]
            dk = jnp.zeros((keys, 128), F32)
            dv = jnp.zeros((keys, 128), F32)
            for j in range(2):
                cols = slice(j * TILE, (j + 1) * TILE)
                w, s = terms(q[cols], o[cols], lse[:, cols], delta[:, cols], k_rows, v_rows, None)
                dv += dot(w, o[cols], (1, 0))
                dk += dot(s, q[cols], (1, 0))
                dq = dq_sum[h, cols] + dot(s, k_rows, (0, 0))
                if i < PARTS - 1:
                    dq_sum[h, cols] = dq
                else:
                    part = (dq * SCALE).astype(BF16).reshape(4, 64, 128)
                    dq_out[j * 4 : (j + 1) * 4, :, h * 128 : (h + 1) * 128] = part
            part = jnp.concatenate([dk * SCALE, dv], axis=1).astype(BF16)
            gate_out[i, :, h] = part.reshape(8, PART, 256)
        for k in (7, 6, 5, 4, 3, 2, 1):
            to, p = me.row(k)
            start(
                remote(gate_out.at[i, p], gate_in.at[i, me.m], b_send.at[i, k], b_recv.at[i, k], to)
            )
        gate_in[i, me.m] = gate_out[i, me.m]
    for k in range(1, 8):
        to, s, _ = me.inner(k)
        start(remote(dq_out.at[s], out_q.at[:, my_cols], g_send.at[k], g_recv.at[k], to))
    dq_local = pltpu.make_async_copy(dq_out.at[me.s], out_q.at[:, my_cols], l_sem.at[0])
    dq_local.start()

    def add_up(i):
        for k in range(1, 8):
            _, p = me.row(k)
            await_part(gate_in.at[i, p], b_send.at[i, k], b_recv.at[i, k])

        def add(j, carry):
            run[i, j] = gate_in[i, j // 4, lax.rem(j, 4)].astype(F32) + run[i, tab[1, j]]
            return carry

        lax.fori_loop(0, 32, add, 0)

    def total(i, d, w):
        return run[i, tab[2, lax.rem(d + 8, 8) * 4 + w]]

    HOPS = (1, 2, 1, 2)

    def sum_on(way, t, i):
        sign = 1 - 2 * way
        first, count = span(way, t)
        for w in range(first, first + count):
            value = total(i, me.z + sign * (t + 1), w)
            if t == 1:
                value += z_in[way, 2, i, w].astype(F32)
                if way * 2 <= w < way * 2 + 2:
                    value += z_in[way, 3, i, w].astype(F32)
            z_out[way, t, i, w] = value.astype(BF16)
        src = z_out.at[way, t, i, pl.ds(first, count)]
        dst = z_in.at[way, t, i, pl.ds(first, count)]
        to = me.plane(sign * HOPS[t])
        start(remote(src, dst, s_send.at[way, t, i], s_recv.at[way, t, i], to))

    def sum_arrived(way, t, i):
        part = z_in.at[way, t, i, pl.ds(*span(way, t))]
        await_part(part, s_send.at[way, t, i], s_recv.at[way, t, i])

    def middle(i):
        for way in range(2):
            sum_arrived(way, 2, i)
            sum_arrived(way, 3, i)
            sum_on(way, 1, i)

    def sum_here(i):
        for t in range(2):
            both(sum_arrived, t, i)
        for w in range(4):
            value = total(i, me.z, w)
            for way in range(2):
                value += z_in[way, 0, i, w].astype(F32) + z_in[way, 1, i, w].astype(F32)
            end_out[i, w] = value
            copy = remote(
                end_out.at[i, w],
                end_in.at[me.g, i],
                e_send.at[w, i],
                e_recv.at[me.g, i],
                me.owner(w),
            )

            def keep():
                end_in[0, i] = end_out[i, w]

            start(copy, staying & (slot == w), keep)

    for i in range(PARTS):
        add_up(i)
        for t in (2, 3, 0):
            both(sum_on, t, i)
        if i >= 1:
            middle(i - 1)
        if i >= 3:
            sum_here(i - 3)
    middle(PARTS - 1)
    for i in range(PARTS - 3, PARTS):
        sum_here(i)

    for k in range(1, 8):
        _, _, e = me.inner(k)
        await_part(own_in.at[e], q_send.at[3, k], q_recv.at[3, k])
    for i in range(PARTS):
        toks = slice(i * PART, (i + 1) * PART)
        for g in range(4):
            value = own_in[2 * g, toks].astype(F32) + own_in[2 * g + 1, toks].astype(F32)
            here = staying if g == 0 else None
            await_part(end_in.at[g, i], e_send.at[g, i], e_recv.at[g, i], here)
            value += end_in[g, i]
            out_k[toks, g * 128 : (g + 1) * 128] = value[:, :128].astype(BF16)
            out_v[toks, g * 128 : (g + 1) * 128] = value[:, 128:].astype(BF16)

    dq_local.wait()
    for k in range(1, 8):
        _, _, e = me.inner(k)
        part = out_q.at[:, pl.ds(pl.multiple_of(e * 512, 512), 512)]
        await_part(part, g_send.at[k], g_recv.at[k])
    for here, copy in maybe_sent:

        @pl.when(jnp.logical_not(here))
        def _():
            copy.wait_send()

    for copy in sent:
        copy.wait_send()


def hand_over(q, k, v, out_q, out_k, out_v, held_q, held_k, held_v, in_sem, out_sem):
    jobs = []
    for i in range(4):
        rows = pl.ds(i * 16, 16)
        jobs.append((q.at[rows], held_q.at[rows], out_q.at[rows]))
    jobs += [(k, held_k, out_k), (v, held_v, out_v)]
    arrivals = [pltpu.make_async_copy(a, b, in_sem.at[i]) for i, (a, b, _) in enumerate(jobs)]
    leavings = [pltpu.make_async_copy(b, c, out_sem.at[i]) for i, (_, b, c) in enumerate(jobs)]
    for copy in arrivals:
        copy.start()
    for arrival, leaving in zip(arrivals, leavings):
        arrival.wait()
        leaving.start()
    for copy in leavings:
        copy.wait()


def vmem(count):
    return [pl.BlockSpec(memory_space=pltpu.VMEM)] * count


SMEM_SPEC = pl.BlockSpec(memory_space=pltpu.SMEM)
HBM_SPEC = pl.BlockSpec(memory_space=pltpu.HBM)
DMA = pltpu.SemaphoreType.DMA
VMEM_LIMIT = 63 * 1024 * 1024


def shape(*dims, dtype=BF16):
    return jax.ShapeDtypeStruct(dims, dtype)


def shards(queries, keys, values, out_grad, lse, delta, gate_block):
    def buf(*dims, dtype=BF16):
        return pltpu.VMEM(dims, dtype)

    parts = pl.pallas_call(
        kernel,
        out_shape=(shape(64, 4096), shape(64, 512), shape(64, 512)),
        in_specs=[SMEM_SPEC, HBM_SPEC, HBM_SPEC] + vmem(4),
        out_specs=(HBM_SPEC, *vmem(2)),
        scratch_shapes=[
            pltpu.SMEM((3, 32), jnp.int32),
            buf(16, 256, dtype=F32),
            buf(8, 64, 512),
            buf(8, 64, 512),
            buf(8, 64, 256),
            buf(2, 16, 256, dtype=F32),
            buf(4, 64, 256),
            *[buf(32, PART, 256) for _ in range(PARTS)],
            buf(PARTS, 8, 4, PART, 256),
            buf(PARTS, 8, 4, PART, 256),
            buf(PARTS, 8, 4, PART, 256),
            buf(PARTS, 8, 4, PART, 256),
            buf(8, 64, 256),
            buf(8, 64, 256),
            buf(4, 512, 128, dtype=F32),
            buf(8, 64, 512),
            buf(PARTS, 33, PART, 256, dtype=F32),
            buf(2, 4, PARTS, 4, PART, 256),
            buf(2, 4, PARTS, 4, PART, 256),
            buf(PARTS, 4, PART, 256, dtype=F32),
            buf(4, PARTS, PART, 256, dtype=F32),
            DMA((4, 8)),
            DMA((4, 8)),
            DMA((2,)),
            DMA((2,)),
            DMA((3, 4, PARTS)),
            DMA((3, 4, PARTS)),
            DMA((2, 4, PARTS)),
            DMA((2, 4, PARTS)),
            DMA((PARTS, 8)),
            DMA((PARTS, 8)),
            DMA((PARTS, 8)),
            DMA((PARTS, 8)),
            DMA((8,)),
            DMA((8,)),
            DMA((2, 4, PARTS)),
            DMA((2, 4, PARTS)),
            DMA((4, PARTS)),
            DMA((4, PARTS)),
            DMA((2,)),
        ],
        compiler_params=pltpu.CompilerParams(
            collective_id=0, has_side_effects=True, vmem_limit_bytes=VMEM_LIMIT
        ),
        name="block_attention_backward",
    )(gate_block, queries, out_grad, keys, values, lse.T, delta.T)
    return pl.pallas_call(
        hand_over,
        out_shape=(shape(64, 4096), shape(64, 512), shape(64, 512)),
        in_specs=[HBM_SPEC] * 3,
        out_specs=(HBM_SPEC,) * 3,
        scratch_shapes=[buf(64, 4096), buf(64, 512), buf(64, 512), DMA((6,)), DMA((6,))],
        compiler_params=pltpu.CompilerParams(vmem_limit_bytes=VMEM_LIMIT),
        name="hand_over",
    )(*parts)


def solution(mesh):
    rows = P(("ctx", "head"), None)
    return jax.shard_map(
        shards,
        mesh=mesh,
        in_specs=(rows, rows, rows, rows, P("ctx", "head"), P("ctx", "head"), P()),
        out_specs=(rows, rows, rows),
        check_vma=False,
    )
```

```python
import math

import jax
import jax.numpy as jnp
from jax import lax
from jax.experimental import pallas as pl
from jax.experimental.pallas import tpu as pltpu
from jax.sharding import PartitionSpec as P

MESH = pl.DeviceIdType.MESH
LOG2E = math.log2(math.e)
SCALE = 1.0 / math.sqrt(128.0)
F32 = jnp.float32
BF16 = jnp.bfloat16
PARTS = 4
PART = 64 // PARTS
GROUPS = ((0,), (1,), (2, 3))
HALF = 32


def flip(bit, by):
    return bit if by == 0 else 1 - bit


def xor(a, b):
    return lax.rem(a + b, 2)


class Place:
    def __init__(self):
        ctx, head = lax.axis_index("ctx"), lax.axis_index("head")
        self.z = ctx // 8
        self.X = lax.rem(ctx // 4, 2)
        self.Y = lax.rem(ctx // 2, 2)
        self.yl = lax.rem(ctx, 2)
        self.xl = head // 2
        self.c = lax.rem(head, 2)
        self.gx, self.gy = xor(self.xl, self.X), xor(self.yl, self.Y)
        self.g = self.gx * 2 + self.gy
        self.e = self.g * 2 + self.c
        self.s = self.yl * 4 + self.xl * 2 + self.c
        self.m = self.X * 4 + self.Y * 2 + self.c
        self.b = self.z * 4 + self.X * 2 + self.Y

    def inner(self, k):
        yl, xl, c = flip(self.yl, k // 4), flip(self.xl, k // 2 % 2), flip(self.c, k % 2)
        e = (xor(xl, self.X) * 2 + xor(yl, self.Y)) * 2 + c
        return device(self.z, self.X, xl, self.Y, yl, c), yl * 4 + xl * 2 + c, e

    def row(self, k):
        X, Y, c = flip(self.X, k // 4), flip(self.Y, k // 2 % 2), flip(self.c, k % 2)
        return device(self.z, X, xor(self.gx, X), Y, xor(self.gy, Y), c), X * 4 + Y * 2 + c

    def taker(self, step, g):
        z = lax.rem(self.z + step + 8, 8)
        return device(z, self.xl, xor(self.xl, g // 2), self.yl, xor(self.yl, g % 2), self.c)

    def owner(self, w, step=0):
        return device(lax.rem(self.z + step + 8, 8), w // 2, self.X, w % 2, self.Y, self.c)

    def plane(self, step):
        return {"ctx": lax.rem(self.z + step + 8, 8) * 8 + self.X * 4 + self.Y * 2 + self.yl}

    def barrier_signal(self, sem):
        for k in range(1, 32):
            to = device(
                self.z,
                flip(self.X, k // 16),
                flip(self.xl, k // 8 % 2),
                flip(self.Y, k // 4 % 2),
                flip(self.yl, k // 2 % 2),
                flip(self.c, k % 2),
            )
            pl.semaphore_signal(sem, inc=1, device_id=to, device_id_type=MESH)
        for step in (1, -1, 2, -2):
            pl.semaphore_signal(sem, inc=1, device_id=self.plane(step), device_id_type=MESH)
        for step in (1, -1, 2, -2):
            for i in range(4):
                to = self.taker(step, i)
                pl.semaphore_signal(sem, inc=1, device_id=to, device_id_type=MESH)
            for i in range(1, 4):
                X, Y = flip(self.xl, i // 2), flip(self.yl, i % 2)
                to = device(lax.rem(self.z + step + 8, 8), X, self.X, Y, self.Y, self.c)
                pl.semaphore_signal(sem, inc=1, device_id=to, device_id_type=MESH)


BARRIER_COUNT = 63


def device(z, X, xl, Y, yl, c):
    return {"ctx": z * 8 + X * 4 + Y * 2 + yl, "head": xl * 2 + c}


def remote(src, dst, send, recv, to):
    return pltpu.make_async_remote_copy(
        src_ref=src, dst_ref=dst, send_sem=send, recv_sem=recv, device_id=to, device_id_type=MESH
    )


def dot(a, b, contract):
    return lax.dot_general(a, b, ((contract[:1], contract[1:]), ((), ())), preferred_element_type=F32)


def terms(q, o, lse, delta, k, v, mask):
    scores = dot(k, q, (1, 1)) * (SCALE * LOG2E)
    weights = jnp.exp2(scores - lse)
    if mask is not None:
        weights = jnp.where(mask, weights, 0.0)
    slopes = weights * (dot(v, o, (1, 1)) - delta)
    return weights.astype(BF16), slopes.astype(BF16)


def kernel(
    gate_hbm,
    q_ref,
    o_ref,
    k_hbm,
    v_hbm,
    l_hbm,
    d_hbm,
    out_q,
    out_k,
    out_v,
    gate_ref,
    tab,
    k_ref,
    v_ref,
    ld_ref,
    sum_k,
    sum_v,
    q_in,
    o_in,
    own_kv,
    ld_in,
    kvl,
    kvz_0,
    kvz_1,
    picked,
    gkv,
    gate_out,
    gate_in,
    own_out,
    own_in,
    dq_sum,
    dq_out,
    run,
    z_out,
    z_in,
    end_out,
    end_in,
    far_in,
    q_send,
    q_recv,
    ld_send,
    ld_recv,
    n_send,
    n_recv,
    z_send,
    z_recv,
    r_send,
    r_recv,
    b_send,
    b_recv,
    g_send,
    g_recv,
    s_send,
    s_recv,
    e_send,
    e_recv,
    f_send,
    f_recv,
    l_sem,
    i_sem,
    o_sem,
):
    kvz = (kvz_0, kvz_1)
    me = Place()
    first = ((k_hbm, k_ref), (v_hbm, v_ref), (gate_hbm, gate_ref))
    first += ((l_hbm, ld_ref.at[pl.ds(0, 8)]), (d_hbm, ld_ref.at[pl.ds(8, 8)]))
    first = [pltpu.make_async_copy(a, b, i_sem.at[n]) for n, (a, b) in enumerate(first)]
    for copy in first:
        copy.start()
    barrier = pltpu.get_barrier_semaphore()
    me.barrier_signal(barrier)
    for i in range(PARTS):
        run[i, 32] = jnp.zeros((PART, 256), F32)
    for copy in first:
        copy.wait()
    for g in range(4):
        kvl[g, :, :128] = k_ref[:, g * 128 : (g + 1) * 128]
        kvl[g, :, 128:] = v_ref[:, g * 128 : (g + 1) * 128]
    pl.semaphore_wait(barrier, BARRIER_COUNT)

    staying = (me.xl == me.X) & (me.yl == me.Y)
    sent = []
    maybe_sent = []

    def start(copy, here=None, local=None):
        if here is None:
            copy.start()
            sent.append(copy)
            return

        @pl.when(here)
        def _():
            local()

        @pl.when(jnp.logical_not(here))
        def _():
            copy.start()

        maybe_sent.append((here, copy))

    def await_part(part, send, recv, here=None):
        copy = remote(part, part, send, recv, me.plane(1))
        if here is None:
            copy.wait_recv()
            return

        @pl.when(jnp.logical_not(here))
        def _():
            copy.wait_recv()

    slot = me.X * 2 + me.Y
    STEPS = (1, -1, 0)
    for i in range(2):
        for n, step in enumerate(STEPS):
            for g in range(4):
                copy = remote(
                    kvl.at[g, pl.ds(i * HALF, HALF)],
                    kvz[i].at[me.b],
                    n_send.at[n, g, i],
                    n_recv.at[n, slot, i],
                    me.taker(step, g),
                )
                if step == 0 and g == 0:

                    def keep():
                        kvz[i][me.b] = kvl[0, i * HALF : (i + 1) * HALF]

                    start(copy, staying, keep)
                else:
                    start(copy)

    for k in range(1, 8):
        to, _, e = me.inner(k)
        start(remote(kvl.at[e // 2], own_kv.at[me.s], q_send.at[2, k], q_recv.at[2, k], to))
    ld_yl = xor(me.c, me.Y)
    ld_xl = xor(me.xl, me.X)
    for core in range(2):
        to = device(me.z, me.X, ld_xl, me.Y, ld_yl, core)
        here = (ld_xl == me.xl) & (ld_yl == me.yl) & (me.c == core)

        def keep():
            ld_in[me.yl] = ld_ref[...]

        start(
            remote(ld_ref, ld_in.at[me.yl], ld_send.at[core], ld_recv.at[me.yl], to), here, keep
        )
    for k in range(1, 8):
        to, _, e = me.inner(k)
        cols = pl.ds(pl.multiple_of(e * 512, 512), 512)
        for i, (src, dst) in enumerate(((q_ref, q_in), (o_ref, o_in))):
            start(remote(src.at[:, cols], dst.at[me.s], q_send.at[i, k], q_recv.at[i, k], to))
    my_cols = pl.ds(pl.multiple_of(me.e * 512, 512), 512)
    local = [
        pltpu.make_async_copy(src.at[:, my_cols], dst.at[me.s], l_sem.at[i])
        for i, (src, dst) in enumerate(((q_ref, q_in), (o_ref, o_in)))
    ]
    for copy in local:
        copy.start()
    own_kv[me.s] = kvl[me.g]

    def fill(j, carry):
        tab[0, j] = gate_ref[me.z * 4 + j // 8, me.g * 8 + lax.rem(j, 8)]
        return carry

    def link(j, carry):
        mine = tab[0, j]
        previous, last = jnp.int32(32), jnp.int32(32)
        for other in range(32):
            gate = tab[0, other]
            previous = jnp.where((gate == mine) & (other < j), other, previous)
            last = jnp.where(gate == j, other, last)
        tab[1, j] = previous
        tab[2, j] = last
        return carry

    lax.fori_loop(0, 32, fill, 0)
    lax.fori_loop(0, 32, link, 0)

    def chunk(d, i, first, count):
        return kvz[i].at[pl.ds(lax.rem(d + 8, 8) * 4 + first, count)]

    def span(way, t):
        return (way * 2, 2) if t == 3 else (0, 4)

    def pass_on(way, t, i):
        sign = 1 - 2 * way
        part = chunk(me.z - sign * t, i, *span(way, t))
        start(remote(part, part, z_send.at[way, t, i], z_recv.at[way, t, i], me.plane(sign)))

    def arrived(way, t, i):
        part = chunk(me.z - (1 - 2 * way) * (t + 1), i, *span(way, t))
        await_part(part, z_send.at[way, t, i], z_recv.at[way, t, i])

    def arrived_first(n, i):
        for w in range(4):
            block = kvz[i].at[lax.rem(me.z - STEPS[n] + 8, 8) * 4 + w]
            here = staying & (slot == w) if n == 2 else None
            await_part(block, n_send.at[n, 0, i], n_recv.at[n, w, i], here)

    def pick(i):
        for k in (7, 6, 5, 4, 3, 2, 1, 0):
            to, p = me.row(k)
            for h in range(4):
                got = kvz[i // 2][tab[0, p * 4 + h], i % 2 * PART : (i % 2 + 1) * PART]
                if k == 0:
                    gkv[i, me.m, h] = got
                else:
                    picked[i, k, h] = got
            if k:
                start(
                    remote(picked.at[i, k], gkv.at[i, me.m], r_send.at[i, k], r_recv.at[i, k], to)
                )

    def both(what, *args):
        for way in range(2):
            what(*args[:-2], way, *args[-2:])

    for i in range(2):
        for way in range(2):
            arrived_first(way, i)
            pass_on(way, 1, i)
    for t in (2, 3):
        for i in range(2):
            for way in range(2):
                arrived(way, t - 1, i)
                pass_on(way, t, i)
    for i in range(2):
        arrived_first(2, i)
        both(arrived, 3, i)
        pick(2 * i)
        pick(2 * i + 1)

    for copy in local:
        copy.wait()
    for k in range(1, 8):
        _, s, _ = me.inner(k)
        for i, dst in enumerate((q_in, o_in, own_kv)):
            await_part(dst.at[s], q_send.at[i, k], q_recv.at[i, k])
    for yl in range(2):
        here = (me.gx == me.xl) & (me.gy == me.c) & (me.yl == yl)
        await_part(ld_in.at[yl], ld_send.at[0], ld_recv.at[yl], here)

    def rows_of(h):
        row = 4 * me.c + h
        lse = jnp.concatenate([ld_in[i, pl.ds(row, 1), :] for i in range(2)], axis=1) * LOG2E
        delta = jnp.concatenate([ld_in[i, pl.ds(row + 8, 1), :] for i in range(2)], axis=1)
        lanes = slice(h * 128, (h + 1) * 128)
        q = q_in[:, :, lanes].reshape(512, 128)
        o = o_in[:, :, lanes].reshape(512, 128)
        return q, o, lse, delta

    TILE = 256
    key_pos = lax.broadcasted_iota(jnp.int32, (TILE, TILE), 0)
    query_pos = lax.broadcasted_iota(jnp.int32, (TILE, TILE), 1)
    causal = key_pos <= query_pos
    own = own_kv[...].reshape(512, 256)
    own_k, own_v = own[:, :128], own[:, 128:]
    own_dk = [jnp.zeros((TILE, 128), F32) for _ in range(2)]
    own_dv = [jnp.zeros((TILE, 128), F32) for _ in range(2)]
    for h in range(4):
        q, o, lse, delta = rows_of(h)
        for i in range(2):
            cols = slice(i * TILE, (i + 1) * TILE)
            dq = jnp.zeros((TILE, 128), F32)
            for j in range(i + 1):
                keys = slice(j * TILE, (j + 1) * TILE)
                mask = causal if i == j else None
                w, s = terms(
                    q[cols], o[cols], lse[:, cols], delta[:, cols], own_k[keys], own_v[keys], mask
                )
                own_dv[j] += dot(w, o[cols], (1, 0))
                own_dk[j] += dot(s, q[cols], (1, 0))
                dq += dot(s, own_k[keys], (0, 0))
            dq_sum[h, cols] = dq
    for j in range(2):
        part = jnp.concatenate([own_dk[j] * SCALE, own_dv[j]], axis=1).astype(BF16)
        own_out[j * 4 : (j + 1) * 4] = part.reshape(4, 64, 256)
    for k in range(1, 8):
        to, s, _ = me.inner(k)
        start(remote(own_out.at[s], own_in.at[me.e], q_send.at[3, k], q_recv.at[3, k], to))
    own_in[me.e] = own_out[me.s]

    keys = 8 * PART
    for group in GROUPS:
        for part in group:
            for k in range(1, 8):
                _, p = me.row(k)
                await_part(gkv.at[part, p], r_send.at[part, k], r_recv.at[part, k])
        for h in range(4):
            q, o, lse, delta = rows_of(h)
            lse = jnp.where(tab[0, me.m * 4 + h] != me.b, lse, 1e30)
            kv = [gkv[part, :, h].reshape(keys, 256) for part in group]
            kv = kv[0] if len(kv) == 1 else jnp.concatenate(kv, axis=0)
            k_rows, v_rows = kv[:, :128], kv[:, 128:]
            dk = jnp.zeros((len(group) * keys, 128), F32)
            dv = jnp.zeros((len(group) * keys, 128), F32)
            for j in range(2):
                cols = slice(j * TILE, (j + 1) * TILE)
                w, s = terms(q[cols], o[cols], lse[:, cols], delta[:, cols], k_rows, v_rows, None)
                dv += dot(w, o[cols], (1, 0))
                dk += dot(s, q[cols], (1, 0))
                dq = dq_sum[h, cols] + dot(s, k_rows, (0, 0))
                if group[-1] < PARTS - 1:
                    dq_sum[h, cols] = dq
                else:
                    piece = (dq * SCALE).astype(BF16).reshape(4, 64, 128)
                    dq_out[j * 4 : (j + 1) * 4, :, h * 128 : (h + 1) * 128] = piece
            both_k_v = jnp.concatenate([dk * SCALE, dv], axis=1).astype(BF16)
            for n, part in enumerate(group):
                gate_out[part, :, h] = both_k_v[n * keys : (n + 1) * keys].reshape(8, PART, 256)
        for part in group:
            for k in (7, 6, 5, 4, 3, 2, 1):
                to, p = me.row(k)
                src, dst = gate_out.at[part, p], gate_in.at[part, me.m]
                start(remote(src, dst, b_send.at[part, k], b_recv.at[part, k], to))
            gate_in[part, me.m] = gate_out[part, me.m]
    for k in range(1, 8):
        to, s, _ = me.inner(k)
        start(remote(dq_out.at[s], out_q.at[:, my_cols], g_send.at[k], g_recv.at[k], to))
    dq_local = pltpu.make_async_copy(dq_out.at[me.s], out_q.at[:, my_cols], l_sem.at[0])
    dq_local.start()

    def add_up(i):
        for k in range(1, 8):
            _, p = me.row(k)
            await_part(gate_in.at[i, p], b_send.at[i, k], b_recv.at[i, k])

        def add(j, carry):
            run[i, j] = gate_in[i, j // 4, lax.rem(j, 4)].astype(F32) + run[i, tab[1, j]]
            return carry

        lax.fori_loop(0, 32, add, 0)

    def total(i, d, w):
        return run[i, tab[2, lax.rem(d + 8, 8) * 4 + w]]

    HOPS = (1, 2, 1, 2)

    def sum_on(way, t, i):
        sign = 1 - 2 * way
        first, count = span(way, t)
        for w in range(first, first + count):
            value = total(i, me.z + sign * (t + 1), w)
            if t == 1:
                value += z_in[way, 2, i, w].astype(F32)
                if way * 2 <= w < way * 2 + 2:
                    value += z_in[way, 3, i, w].astype(F32)
            z_out[way, t, i, w] = value.astype(BF16)
        if t < 2 and i == PARTS - 1:
            for w in range(4):
                dst = far_in.at[way, t, me.g]
                to = me.owner(w, sign * HOPS[t])
                start(
                    remote(z_out.at[way, t, i, w], dst, f_send.at[way, t, w], f_recv.at[way, t, me.g], to)
                )
            return
        src = z_out.at[way, t, i, pl.ds(first, count)]
        dst = z_in.at[way, t, i, pl.ds(first, count)]
        to = me.plane(sign * HOPS[t])
        start(remote(src, dst, s_send.at[way, t, i], s_recv.at[way, t, i], to))

    def sum_arrived(way, t, i):
        part = z_in.at[way, t, i, pl.ds(*span(way, t))]
        await_part(part, s_send.at[way, t, i], s_recv.at[way, t, i])

    def middle(i):
        for way in range(2):
            sum_arrived(way, 2, i)
            sum_arrived(way, 3, i)
            sum_on(way, 1, i)

    def sum_here(i):
        far = i == PARTS - 1
        for t in range(0 if far else 2):
            both(sum_arrived, t, i)
        for w in range(4):
            value = total(i, me.z, w)
            for way in range(0 if far else 2):
                value += z_in[way, 0, i, w].astype(F32) + z_in[way, 1, i, w].astype(F32)
            end_out[i, w] = value
            copy = remote(
                end_out.at[i, w],
                end_in.at[me.g, i],
                e_send.at[w, i],
                e_recv.at[me.g, i],
                me.owner(w),
            )

            def keep():
                end_in[0, i] = end_out[i, w]

            start(copy, staying & (slot == w), keep)

    for i in range(PARTS):
        add_up(i)
        for t in (2, 3, 0):
            both(sum_on, t, i)
        if i >= 1:
            middle(i - 1)
        if i >= 3:
            sum_here(i - 3)
    sum_here(PARTS - 1)
    sum_here(PARTS - 3)
    middle(PARTS - 1)
    sum_here(PARTS - 2)

    for k in range(1, 8):
        _, _, e = me.inner(k)
        await_part(own_in.at[e], q_send.at[3, k], q_recv.at[3, k])
    results = []
    for i in range(PARTS):
        toks = slice(i * PART, (i + 1) * PART)
        for g in range(4):
            value = own_in[2 * g, toks].astype(F32) + own_in[2 * g + 1, toks].astype(F32)
            here = staying if g == 0 else None
            await_part(end_in.at[g, i], e_send.at[g, i], e_recv.at[g, i], here)
            value += end_in[g, i]
            if i == PARTS - 1:
                for way in range(2):
                    for t in range(2):
                        part = far_in.at[way, t, g]
                        await_part(part, f_send.at[way, t, g], f_recv.at[way, t, g])
                        value += far_in[way, t, g].astype(F32)
            sum_k[toks, g * 128 : (g + 1) * 128] = value[:, :128].astype(BF16)
            sum_v[toks, g * 128 : (g + 1) * 128] = value[:, 128:].astype(BF16)
        for n, (src, dst) in enumerate(((sum_k, out_k), (sum_v, out_v))):
            rows = pl.ds(i * PART, PART)
            results.append(pltpu.make_async_copy(src.at[rows], dst.at[rows], o_sem.at[n, i]))
            results[-1].start()

    for copy in [dq_local] + results:
        copy.wait()
    for k in range(1, 8):
        _, _, e = me.inner(k)
        part = out_q.at[:, pl.ds(pl.multiple_of(e * 512, 512), 512)]
        await_part(part, g_send.at[k], g_recv.at[k])
    for here, copy in maybe_sent:

        @pl.when(jnp.logical_not(here))
        def _():
            copy.wait_send()

    for copy in sent:
        copy.wait_send()


def hand_over(q, k, v, out_q, out_k, out_v, held_q, held_k, held_v, in_sem, out_sem):
    jobs = []
    for i in range(4):
        rows = pl.ds(i * 16, 16)
        jobs.append((q.at[rows], held_q.at[rows], out_q.at[rows]))
    jobs += [(k, held_k, out_k), (v, held_v, out_v)]
    arrivals = [pltpu.make_async_copy(a, b, in_sem.at[i]) for i, (a, b, _) in enumerate(jobs)]
    leavings = [pltpu.make_async_copy(b, c, out_sem.at[i]) for i, (_, b, c) in enumerate(jobs)]
    for copy in arrivals:
        copy.start()
    for arrival, leaving in zip(arrivals, leavings):
        arrival.wait()
        leaving.start()
    for copy in leavings:
        copy.wait()


HBM_SPEC = pl.BlockSpec(memory_space=pltpu.HBM)
DMA = pltpu.SemaphoreType.DMA
VMEM_LIMIT = 63 * 1024 * 1024


def shape(*dims, dtype=BF16):
    return jax.ShapeDtypeStruct(dims, dtype)


def shards(queries, keys, values, out_grad, lse, delta, gate_block):
    def buf(*dims, dtype=BF16):
        return pltpu.VMEM(dims, dtype)

    parts = pl.pallas_call(
        kernel,
        out_shape=(shape(64, 4096), shape(64, 512), shape(64, 512)),
        in_specs=[HBM_SPEC] * 7,
        out_specs=(HBM_SPEC,) * 3,
        scratch_shapes=[
            pltpu.SMEM((32, 32), jnp.int32),
            pltpu.SMEM((3, 32), jnp.int32),
            buf(64, 512),
            buf(64, 512),
            buf(16, 256, dtype=F32),
            buf(64, 512),
            buf(64, 512),
            buf(8, 64, 512),
            buf(8, 64, 512),
            buf(8, 64, 256),
            buf(2, 16, 256, dtype=F32),
            buf(4, 64, 256),
            buf(32, HALF, 256),
            buf(32, HALF, 256),
            buf(PARTS, 8, 4, PART, 256),
            buf(PARTS, 8, 4, PART, 256),
            buf(PARTS, 8, 4, PART, 256),
            buf(PARTS, 8, 4, PART, 256),
            buf(8, 64, 256),
            buf(8, 64, 256),
            buf(4, 512, 128, dtype=F32),
            buf(8, 64, 512),
            buf(PARTS, 33, PART, 256, dtype=F32),
            buf(2, 4, PARTS, 4, PART, 256),
            buf(2, 4, PARTS, 4, PART, 256),
            buf(PARTS, 4, PART, 256, dtype=F32),
            buf(4, PARTS, PART, 256, dtype=F32),
            buf(2, 2, 4, PART, 256),
            DMA((4, 8)),
            DMA((4, 8)),
            DMA((2,)),
            DMA((2,)),
            DMA((3, 4, 2)),
            DMA((3, 4, 2)),
            DMA((2, 4, 2)),
            DMA((2, 4, 2)),
            DMA((PARTS, 8)),
            DMA((PARTS, 8)),
            DMA((PARTS, 8)),
            DMA((PARTS, 8)),
            DMA((8,)),
            DMA((8,)),
            DMA((2, 4, PARTS)),
            DMA((2, 4, PARTS)),
            DMA((4, PARTS)),
            DMA((4, PARTS)),
            DMA((2, 2, 4)),
            DMA((2, 2, 4)),
            DMA((2,)),
            DMA((5,)),
            DMA((2, PARTS)),
        ],
        compiler_params=pltpu.CompilerParams(
            collective_id=0, has_side_effects=True, vmem_limit_bytes=VMEM_LIMIT
        ),
        name="block_attention_backward",
    )(gate_block, queries, out_grad, keys, values, lse.T, delta.T)
    return pl.pallas_call(
        hand_over,
        out_shape=(shape(64, 4096), shape(64, 512), shape(64, 512)),
        in_specs=[HBM_SPEC] * 3,
        out_specs=(HBM_SPEC,) * 3,
        scratch_shapes=[buf(64, 4096), buf(64, 512), buf(64, 512), DMA((6,)), DMA((6,))],
        compiler_params=pltpu.CompilerParams(vmem_limit_bytes=VMEM_LIMIT),
        name="hand_over",
    )(*parts)


def solution(mesh):
    rows = P(("ctx", "head"), None)
    return jax.shard_map(
        shards,
        mesh=mesh,
        in_specs=(rows, rows, rows, rows, P("ctx", "head"), P("ctx", "head"), P()),
        out_specs=(rows, rows, rows),
        check_vma=False,
    )
```

```python
import math

import jax
import jax.numpy as jnp
from jax import lax
from jax.experimental import pallas as pl
from jax.experimental.pallas import tpu as pltpu
from jax.sharding import PartitionSpec as P

MESH = pl.DeviceIdType.MESH
LOG2E = math.log2(math.e)
SCALE = 1.0 / math.sqrt(128.0)
F32 = jnp.float32
BF16 = jnp.bfloat16
PARTS = 4
PART = 64 // PARTS
GROUPS = ((0,), (1,), (2, 3))
HALF = 32


def flip(bit, by):
    return bit if by == 0 else 1 - bit


def xor(a, b):
    return lax.rem(a + b, 2)


class Place:
    def __init__(self):
        ctx, head = lax.axis_index("ctx"), lax.axis_index("head")
        self.z = ctx // 8
        self.X = lax.rem(ctx // 4, 2)
        self.Y = lax.rem(ctx // 2, 2)
        self.yl = lax.rem(ctx, 2)
        self.xl = head // 2
        self.c = lax.rem(head, 2)
        self.gx, self.gy = xor(self.xl, self.X), xor(self.yl, self.Y)
        self.g = self.gx * 2 + self.gy
        self.e = self.g * 2 + self.c
        self.s = self.yl * 4 + self.xl * 2 + self.c
        self.m = self.X * 4 + self.Y * 2 + self.c
        self.b = self.z * 4 + self.X * 2 + self.Y

    def inner(self, k):
        yl, xl, c = flip(self.yl, k // 4), flip(self.xl, k // 2 % 2), flip(self.c, k % 2)
        e = (xor(xl, self.X) * 2 + xor(yl, self.Y)) * 2 + c
        return device(self.z, self.X, xl, self.Y, yl, c), yl * 4 + xl * 2 + c, e

    def row(self, k):
        X, Y, c = flip(self.X, k // 4), flip(self.Y, k // 2 % 2), flip(self.c, k % 2)
        return device(self.z, X, xor(self.gx, X), Y, xor(self.gy, Y), c), X * 4 + Y * 2 + c

    def taker(self, step, g):
        z = lax.rem(self.z + step + 8, 8)
        return device(z, self.xl, xor(self.xl, g // 2), self.yl, xor(self.yl, g % 2), self.c)

    def owner(self, w, step=0):
        return device(lax.rem(self.z + step + 8, 8), w // 2, self.X, w % 2, self.Y, self.c)

    def plane(self, step):
        return {"ctx": lax.rem(self.z + step + 8, 8) * 8 + self.X * 4 + self.Y * 2 + self.yl}

    def barrier(self):
        sem = pltpu.get_barrier_semaphore()

        def greet(to):
            pl.semaphore_signal(sem, inc=1, device_id=to, device_id_type=MESH)

        for step in (2, -2, 1, -1, 0):
            z = lax.rem(self.z + step + 8, 8)
            for i in range(1, 4):
                greet(device(z, self.xl, flip(self.X, i // 2), self.yl, flip(self.Y, i % 2), self.c))
                greet(device(z, flip(self.xl, i // 2), self.X, flip(self.yl, i % 2), self.Y, self.c))
            if step:
                greet(device(z, self.xl, self.X, self.yl, self.Y, self.c))
                greet(self.plane(step))
        for k in range(2, 8):
            greet(self.row(k)[0])
        for k in range(1, 8):
            greet(self.inner(k)[0])
        swapped = device(self.z, self.xl, self.X, self.yl, self.Y, self.c)
        here = (self.xl == self.X) & (self.yl == self.Y)

        @pl.when(jnp.logical_not(here))
        def _():
            greet(swapped)

        return lambda: pl.semaphore_wait(sem, 52 - here.astype(jnp.int32))


def device(z, X, xl, Y, yl, c):
    return {"ctx": z * 8 + X * 4 + Y * 2 + yl, "head": xl * 2 + c}


def remote(src, dst, send, recv, to):
    return pltpu.make_async_remote_copy(
        src_ref=src, dst_ref=dst, send_sem=send, recv_sem=recv, device_id=to, device_id_type=MESH
    )


def dot(a, b, contract):
    return lax.dot_general(a, b, ((contract[:1], contract[1:]), ((), ())), preferred_element_type=F32)


def terms(q, o, lse, delta, k, v, mask):
    scores = dot(k, q, (1, 1)) * (SCALE * LOG2E)
    weights = jnp.exp2(scores - lse)
    if mask is not None:
        weights = jnp.where(mask, weights, 0.0)
    slopes = weights * (dot(v, o, (1, 1)) - delta)
    return weights.astype(BF16), slopes.astype(BF16)


def kernel(
    gate_hbm,
    q_ref,
    o_ref,
    k_hbm,
    v_hbm,
    l_hbm,
    d_hbm,
    out_q,
    out_k,
    out_v,
    gate_ref,
    tab,
    k_ref,
    v_ref,
    ld_ref,
    sum_k,
    sum_v,
    q_in,
    o_in,
    own_kv,
    ld_in,
    kvl,
    kvz_0,
    kvz_1,
    picked,
    gkv,
    gate_out,
    gate_in,
    own_out,
    own_in,
    dq_sum,
    dq_out,
    run,
    z_out,
    z_in,
    end_out,
    end_in,
    far_in,
    q_send,
    q_recv,
    ld_send,
    ld_recv,
    n_send,
    n_recv,
    z_send,
    z_recv,
    r_send,
    r_recv,
    b_send,
    b_recv,
    g_send,
    g_recv,
    s_send,
    s_recv,
    e_send,
    e_recv,
    f_send,
    f_recv,
    l_sem,
    i_sem,
    o_sem,
):
    kvz = (kvz_0, kvz_1)
    me = Place()
    first = ((k_hbm, k_ref), (v_hbm, v_ref), (gate_hbm, gate_ref))
    first += ((l_hbm, ld_ref.at[pl.ds(0, 8)]), (d_hbm, ld_ref.at[pl.ds(8, 8)]))
    first = [pltpu.make_async_copy(a, b, i_sem.at[n]) for n, (a, b) in enumerate(first)]
    for copy in first:
        copy.start()
    everyone_is_here = me.barrier()
    for i in range(PARTS):
        run[i, 32] = jnp.zeros((PART, 256), F32)
    for copy in first:
        copy.wait()
    for g in range(4):
        kvl[g, :, :128] = k_ref[:, g * 128 : (g + 1) * 128]
        kvl[g, :, 128:] = v_ref[:, g * 128 : (g + 1) * 128]
    everyone_is_here()

    staying = (me.xl == me.X) & (me.yl == me.Y)
    sent = []
    maybe_sent = []

    def start(copy, here=None, local=None):
        if here is None:
            copy.start()
            sent.append(copy)
            return

        @pl.when(here)
        def _():
            local()

        @pl.when(jnp.logical_not(here))
        def _():
            copy.start()

        maybe_sent.append((here, copy))

    def await_part(part, send, recv, here=None):
        copy = remote(part, part, send, recv, me.plane(1))
        if here is None:
            copy.wait_recv()
            return

        @pl.when(jnp.logical_not(here))
        def _():
            copy.wait_recv()

    slot = me.X * 2 + me.Y
    STEPS = (1, -1, 0)
    for i in range(2):
        for n, step in enumerate(STEPS):
            for g in range(4):
                copy = remote(
                    kvl.at[g, pl.ds(i * HALF, HALF)],
                    kvz[i].at[me.b],
                    n_send.at[n, g, i],
                    n_recv.at[n, slot, i],
                    me.taker(step, g),
                )
                if step == 0 and g == 0:

                    def keep():
                        kvz[i][me.b] = kvl[0, i * HALF : (i + 1) * HALF]

                    start(copy, staying, keep)
                else:
                    start(copy)

    for k in range(1, 8):
        to, _, e = me.inner(k)
        start(remote(kvl.at[e // 2], own_kv.at[me.s], q_send.at[2, k], q_recv.at[2, k], to))
    ld_yl = xor(me.c, me.Y)
    ld_xl = xor(me.xl, me.X)
    for core in range(2):
        to = device(me.z, me.X, ld_xl, me.Y, ld_yl, core)
        here = (ld_xl == me.xl) & (ld_yl == me.yl) & (me.c == core)

        def keep():
            ld_in[me.yl] = ld_ref[...]

        start(
            remote(ld_ref, ld_in.at[me.yl], ld_send.at[core], ld_recv.at[me.yl], to), here, keep
        )
    for k in range(1, 8):
        to, _, e = me.inner(k)
        cols = pl.ds(pl.multiple_of(e * 512, 512), 512)
        for i, (src, dst) in enumerate(((q_ref, q_in), (o_ref, o_in))):
            start(remote(src.at[:, cols], dst.at[me.s], q_send.at[i, k], q_recv.at[i, k], to))
    my_cols = pl.ds(pl.multiple_of(me.e * 512, 512), 512)
    local = [
        pltpu.make_async_copy(src.at[:, my_cols], dst.at[me.s], l_sem.at[i])
        for i, (src, dst) in enumerate(((q_ref, q_in), (o_ref, o_in)))
    ]
    for copy in local:
        copy.start()
    own_kv[me.s] = kvl[me.g]

    def fill(j, carry):
        tab[0, j] = gate_ref[me.z * 4 + j // 8, me.g * 8 + lax.rem(j, 8)]
        return carry

    def link(j, carry):
        mine = tab[0, j]
        previous, last = jnp.int32(32), jnp.int32(32)
        for other in range(32):
            gate = tab[0, other]
            previous = jnp.where((gate == mine) & (other < j), other, previous)
            last = jnp.where(gate == j, other, last)
        tab[1, j] = previous
        tab[2, j] = last
        return carry

    lax.fori_loop(0, 32, fill, 0)

    def chunk(d, i, first, count):
        return kvz[i].at[pl.ds(lax.rem(d + 8, 8) * 4 + first, count)]

    def span(way, t):
        return (way * 2, 2) if t == 3 else (0, 4)

    def pass_on(way, t, i):
        sign = 1 - 2 * way
        part = chunk(me.z - sign * t, i, *span(way, t))
        start(remote(part, part, z_send.at[way, t, i], z_recv.at[way, t, i], me.plane(sign)))

    def arrived(way, t, i):
        part = chunk(me.z - (1 - 2 * way) * (t + 1), i, *span(way, t))
        await_part(part, z_send.at[way, t, i], z_recv.at[way, t, i])

    def arrived_first(n, i):
        for w in range(4):
            block = kvz[i].at[lax.rem(me.z - STEPS[n] + 8, 8) * 4 + w]
            here = staying & (slot == w) if n == 2 else None
            await_part(block, n_send.at[n, 0, i], n_recv.at[n, w, i], here)

    def pick(i):
        for k in (7, 6, 5, 4, 3, 2, 1, 0):
            to, p = me.row(k)
            for h in range(4):
                got = kvz[i // 2][tab[0, p * 4 + h], i % 2 * PART : (i % 2 + 1) * PART]
                if k == 0:
                    gkv[i, me.m, h] = got
                else:
                    picked[i, k, h] = got
            if k:
                start(
                    remote(picked.at[i, k], gkv.at[i, me.m], r_send.at[i, k], r_recv.at[i, k], to)
                )

    def both(what, *args):
        for way in range(2):
            what(*args[:-2], way, *args[-2:])

    for i in range(2):
        for way in range(2):
            arrived_first(way, i)
            pass_on(way, 1, i)
    for t in (2, 3):
        for i in range(2):
            for way in range(2):
                arrived(way, t - 1, i)
                pass_on(way, t, i)
    for i in range(2):
        arrived_first(2, i)
        both(arrived, 3, i)
        pick(2 * i)
        pick(2 * i + 1)
    lax.fori_loop(0, 32, link, 0)

    for copy in local:
        copy.wait()
    for k in range(1, 8):
        _, s, _ = me.inner(k)
        for i, dst in enumerate((q_in, o_in, own_kv)):
            await_part(dst.at[s], q_send.at[i, k], q_recv.at[i, k])
    for yl in range(2):
        here = (me.gx == me.xl) & (me.gy == me.c) & (me.yl == yl)
        await_part(ld_in.at[yl], ld_send.at[0], ld_recv.at[yl], here)

    def rows_of(h):
        row = 4 * me.c + h
        lse = jnp.concatenate([ld_in[i, pl.ds(row, 1), :] for i in range(2)], axis=1) * LOG2E
        delta = jnp.concatenate([ld_in[i, pl.ds(row + 8, 1), :] for i in range(2)], axis=1)
        lanes = slice(h * 128, (h + 1) * 128)
        q = q_in[:, :, lanes].reshape(512, 128)
        o = o_in[:, :, lanes].reshape(512, 128)
        return q, o, lse, delta

    TILE = 256
    key_pos = lax.broadcasted_iota(jnp.int32, (TILE, TILE), 0)
    query_pos = lax.broadcasted_iota(jnp.int32, (TILE, TILE), 1)
    causal = key_pos <= query_pos
    own = own_kv[...].reshape(512, 256)
    own_k, own_v = own[:, :128], own[:, 128:]
    own_dk = [jnp.zeros((TILE, 128), F32) for _ in range(2)]
    own_dv = [jnp.zeros((TILE, 128), F32) for _ in range(2)]
    for h in range(4):
        q, o, lse, delta = rows_of(h)
        for i in range(2):
            cols = slice(i * TILE, (i + 1) * TILE)
            dq = jnp.zeros((TILE, 128), F32)
            for j in range(i + 1):
                keys = slice(j * TILE, (j + 1) * TILE)
                mask = causal if i == j else None
                w, s = terms(
                    q[cols], o[cols], lse[:, cols], delta[:, cols], own_k[keys], own_v[keys], mask
                )
                own_dv[j] += dot(w, o[cols], (1, 0))
                own_dk[j] += dot(s, q[cols], (1, 0))
                dq += dot(s, own_k[keys], (0, 0))
            dq_sum[h, cols] = dq
    for j in range(2):
        part = jnp.concatenate([own_dk[j] * SCALE, own_dv[j]], axis=1).astype(BF16)
        own_out[j * 4 : (j + 1) * 4] = part.reshape(4, 64, 256)
    for k in range(1, 8):
        to, s, _ = me.inner(k)
        start(remote(own_out.at[s], own_in.at[me.e], q_send.at[3, k], q_recv.at[3, k], to))
    own_in[me.e] = own_out[me.s]

    keys = 8 * PART
    for group in GROUPS:
        for part in group:
            for k in range(1, 8):
                _, p = me.row(k)
                await_part(gkv.at[part, p], r_send.at[part, k], r_recv.at[part, k])
        for h in range(4):
            q, o, lse, delta = rows_of(h)
            lse = jnp.where(tab[0, me.m * 4 + h] != me.b, lse, 1e30)
            kv = [gkv[part, :, h].reshape(keys, 256) for part in group]
            kv = kv[0] if len(kv) == 1 else jnp.concatenate(kv, axis=0)
            k_rows, v_rows = kv[:, :128], kv[:, 128:]
            dk = jnp.zeros((len(group) * keys, 128), F32)
            dv = jnp.zeros((len(group) * keys, 128), F32)
            for j in range(2):
                cols = slice(j * TILE, (j + 1) * TILE)
                w, s = terms(q[cols], o[cols], lse[:, cols], delta[:, cols], k_rows, v_rows, None)
                dv += dot(w, o[cols], (1, 0))
                dk += dot(s, q[cols], (1, 0))
                dq = dq_sum[h, cols] + dot(s, k_rows, (0, 0))
                if group[-1] < PARTS - 1:
                    dq_sum[h, cols] = dq
                else:
                    piece = (dq * SCALE).astype(BF16).reshape(4, 64, 128)
                    dq_out[j * 4 : (j + 1) * 4, :, h * 128 : (h + 1) * 128] = piece
            both_k_v = jnp.concatenate([dk * SCALE, dv], axis=1).astype(BF16)
            for n, part in enumerate(group):
                gate_out[part, :, h] = both_k_v[n * keys : (n + 1) * keys].reshape(8, PART, 256)
        for part in group:
            for k in (7, 6, 5, 4, 3, 2, 1):
                to, p = me.row(k)
                src, dst = gate_out.at[part, p], gate_in.at[part, me.m]
                start(remote(src, dst, b_send.at[part, k], b_recv.at[part, k], to))
            gate_in[part, me.m] = gate_out[part, me.m]
    for k in range(1, 8):
        to, s, _ = me.inner(k)
        start(remote(dq_out.at[s], out_q.at[:, my_cols], g_send.at[k], g_recv.at[k], to))
    dq_local = pltpu.make_async_copy(dq_out.at[me.s], out_q.at[:, my_cols], l_sem.at[0])
    dq_local.start()

    def add_up(i):
        for k in range(1, 8):
            _, p = me.row(k)
            await_part(gate_in.at[i, p], b_send.at[i, k], b_recv.at[i, k])

        def add(j, carry):
            run[i, j] = gate_in[i, j // 4, lax.rem(j, 4)].astype(F32) + run[i, tab[1, j]]
            return carry

        lax.fori_loop(0, 32, add, 0)

    def total(i, d, w):
        return run[i, tab[2, lax.rem(d + 8, 8) * 4 + w]]

    HOPS = (1, 2, 1, 2)

    def sum_on(way, t, i):
        sign = 1 - 2 * way
        first, count = span(way, t)
        for w in range(first, first + count):
            value = total(i, me.z + sign * (t + 1), w)
            if t == 1:
                value += z_in[way, 2, i, w].astype(F32)
                if way * 2 <= w < way * 2 + 2:
                    value += z_in[way, 3, i, w].astype(F32)
            z_out[way, t, i, w] = value.astype(BF16)
        if t < 2 and i == PARTS - 1:
            for w in range(4):
                dst = far_in.at[way, t, me.g]
                to = me.owner(w, sign * HOPS[t])
                start(
                    remote(z_out.at[way, t, i, w], dst, f_send.at[way, t, w], f_recv.at[way, t, me.g], to)
                )
            return
        src = z_out.at[way, t, i, pl.ds(first, count)]
        dst = z_in.at[way, t, i, pl.ds(first, count)]
        to = me.plane(sign * HOPS[t])
        start(remote(src, dst, s_send.at[way, t, i], s_recv.at[way, t, i], to))

    def sum_arrived(way, t, i):
        part = z_in.at[way, t, i, pl.ds(*span(way, t))]
        await_part(part, s_send.at[way, t, i], s_recv.at[way, t, i])

    def middle(i):
        for way in range(2):
            sum_arrived(way, 2, i)
            sum_arrived(way, 3, i)
            sum_on(way, 1, i)

    def sum_here(i):
        far = i == PARTS - 1
        for t in range(0 if far else 2):
            both(sum_arrived, t, i)
        for w in range(4):
            value = total(i, me.z, w)
            for way in range(0 if far else 2):
                value += z_in[way, 0, i, w].astype(F32) + z_in[way, 1, i, w].astype(F32)
            end_out[i, w] = value
            copy = remote(
                end_out.at[i, w],
                end_in.at[me.g, i],
                e_send.at[w, i],
                e_recv.at[me.g, i],
                me.owner(w),
            )

            def keep():
                end_in[0, i] = end_out[i, w]

            start(copy, staying & (slot == w), keep)

    for i in range(PARTS):
        add_up(i)
        for t in (2, 3, 0):
            both(sum_on, t, i)
        if i >= 1:
            middle(i - 1)
        if i >= 3:
            sum_here(i - 3)
    sum_here(PARTS - 1)
    sum_here(PARTS - 3)
    middle(PARTS - 1)
    sum_here(PARTS - 2)

    for k in range(1, 8):
        _, _, e = me.inner(k)
        await_part(own_in.at[e], q_send.at[3, k], q_recv.at[3, k])
    results = []
    for i in range(PARTS):
        toks = slice(i * PART, (i + 1) * PART)
        for g in range(4):
            value = own_in[2 * g, toks].astype(F32) + own_in[2 * g + 1, toks].astype(F32)
            here = staying if g == 0 else None
            await_part(end_in.at[g, i], e_send.at[g, i], e_recv.at[g, i], here)
            value += end_in[g, i]
            if i == PARTS - 1:
                for way in range(2):
                    for t in range(2):
                        part = far_in.at[way, t, g]
                        await_part(part, f_send.at[way, t, g], f_recv.at[way, t, g])
                        value += far_in[way, t, g].astype(F32)
            sum_k[toks, g * 128 : (g + 1) * 128] = value[:, :128].astype(BF16)
            sum_v[toks, g * 128 : (g + 1) * 128] = value[:, 128:].astype(BF16)
        for n, (src, dst) in enumerate(((sum_k, out_k), (sum_v, out_v))):
            rows = pl.ds(i * PART, PART)
            results.append(pltpu.make_async_copy(src.at[rows], dst.at[rows], o_sem.at[n, i]))
            results[-1].start()

    for copy in [dq_local] + results:
        copy.wait()
    for k in range(1, 8):
        _, _, e = me.inner(k)
        part = out_q.at[:, pl.ds(pl.multiple_of(e * 512, 512), 512)]
        await_part(part, g_send.at[k], g_recv.at[k])
    for here, copy in maybe_sent:

        @pl.when(jnp.logical_not(here))
        def _():
            copy.wait_send()

    for copy in sent:
        copy.wait_send()


def hand_over(q, k, v, out_q, out_k, out_v, held_q, held_k, held_v, in_sem, out_sem):
    jobs = []
    for i in range(4):
        rows = pl.ds(i * 16, 16)
        jobs.append((q.at[rows], held_q.at[rows], out_q.at[rows]))
    jobs += [(k, held_k, out_k), (v, held_v, out_v)]
    arrivals = [pltpu.make_async_copy(a, b, in_sem.at[i]) for i, (a, b, _) in enumerate(jobs)]
    leavings = [pltpu.make_async_copy(b, c, out_sem.at[i]) for i, (_, b, c) in enumerate(jobs)]
    for copy in arrivals:
        copy.start()
    for arrival, leaving in zip(arrivals, leavings):
        arrival.wait()
        leaving.start()
    for copy in leavings:
        copy.wait()


HBM_SPEC = pl.BlockSpec(memory_space=pltpu.HBM)
DMA = pltpu.SemaphoreType.DMA
VMEM_LIMIT = 63 * 1024 * 1024


def shape(*dims, dtype=BF16):
    return jax.ShapeDtypeStruct(dims, dtype)


def shards(queries, keys, values, out_grad, lse, delta, gate_block):
    def buf(*dims, dtype=BF16):
        return pltpu.VMEM(dims, dtype)

    parts = pl.pallas_call(
        kernel,
        out_shape=(shape(64, 4096), shape(64, 512), shape(64, 512)),
        in_specs=[HBM_SPEC] * 7,
        out_specs=(HBM_SPEC,) * 3,
        scratch_shapes=[
            pltpu.SMEM((32, 32), jnp.int32),
            pltpu.SMEM((3, 32), jnp.int32),
            buf(64, 512),
            buf(64, 512),
            buf(16, 256, dtype=F32),
            buf(64, 512),
            buf(64, 512),
            buf(8, 64, 512),
            buf(8, 64, 512),
            buf(8, 64, 256),
            buf(2, 16, 256, dtype=F32),
            buf(4, 64, 256),
            buf(32, HALF, 256),
            buf(32, HALF, 256),
            buf(PARTS, 8, 4, PART, 256),
            buf(PARTS, 8, 4, PART, 256),
            buf(PARTS, 8, 4, PART, 256),
            buf(PARTS, 8, 4, PART, 256),
            buf(8, 64, 256),
            buf(8, 64, 256),
            buf(4, 512, 128, dtype=F32),
            buf(8, 64, 512),
            buf(PARTS, 33, PART, 256, dtype=F32),
            buf(2, 4, PARTS, 4, PART, 256),
            buf(2, 4, PARTS, 4, PART, 256),
            buf(PARTS, 4, PART, 256, dtype=F32),
            buf(4, PARTS, PART, 256, dtype=F32),
            buf(2, 2, 4, PART, 256),
            DMA((4, 8)),
            DMA((4, 8)),
            DMA((2,)),
            DMA((2,)),
            DMA((3, 4, 2)),
            DMA((3, 4, 2)),
            DMA((2, 4, 2)),
            DMA((2, 4, 2)),
            DMA((PARTS, 8)),
            DMA((PARTS, 8)),
            DMA((PARTS, 8)),
            DMA((PARTS, 8)),
            DMA((8,)),
            DMA((8,)),
            DMA((2, 4, PARTS)),
            DMA((2, 4, PARTS)),
            DMA((4, PARTS)),
            DMA((4, PARTS)),
            DMA((2, 2, 4)),
            DMA((2, 2, 4)),
            DMA((2,)),
            DMA((5,)),
            DMA((2, PARTS)),
        ],
        compiler_params=pltpu.CompilerParams(
            collective_id=0, has_side_effects=True, vmem_limit_bytes=VMEM_LIMIT
        ),
        name="block_attention_backward",
    )(gate_block, queries, out_grad, keys, values, lse.T, delta.T)
    return pl.pallas_call(
        hand_over,
        out_shape=(shape(64, 4096), shape(64, 512), shape(64, 512)),
        in_specs=[HBM_SPEC] * 3,
        out_specs=(HBM_SPEC,) * 3,
        scratch_shapes=[buf(64, 4096), buf(64, 512), buf(64, 512), DMA((6,)), DMA((6,))],
        compiler_params=pltpu.CompilerParams(vmem_limit_bytes=VMEM_LIMIT),
        name="hand_over",
    )(*parts)


def solution(mesh):
    rows = P(("ctx", "head"), None)
    return jax.shard_map(
        shards,
        mesh=mesh,
        in_specs=(rows, rows, rows, rows, P("ctx", "head"), P("ctx", "head"), P()),
        out_specs=(rows, rows, rows),
        check_vma=False,
    )
```

```python
import math

import jax
import jax.numpy as jnp
from jax import lax
from jax.experimental import pallas as pl
from jax.experimental.pallas import tpu as pltpu
from jax.sharding import PartitionSpec as P

MESH = pl.DeviceIdType.MESH
LOG2E = math.log2(math.e)
SCALE = 1.0 / math.sqrt(128.0)
F32 = jnp.float32
BF16 = jnp.bfloat16
PARTS = 4
PART = 64 // PARTS
GROUPS = ((0,), (1,), (2, 3))
HALF = 32


def flip(bit, by):
    return bit if by == 0 else 1 - bit


def xor(a, b):
    return lax.rem(a + b, 2)


class Place:
    def __init__(self):
        ctx, head = lax.axis_index("ctx"), lax.axis_index("head")
        self.z = ctx // 8
        self.X = lax.rem(ctx // 4, 2)
        self.Y = lax.rem(ctx // 2, 2)
        self.yl = lax.rem(ctx, 2)
        self.xl = head // 2
        self.c = lax.rem(head, 2)
        self.gx, self.gy = xor(self.xl, self.X), xor(self.yl, self.Y)
        self.g = self.gx * 2 + self.gy
        self.e = self.g * 2 + self.c
        self.s = self.yl * 4 + self.xl * 2 + self.c
        self.m = self.X * 4 + self.Y * 2 + self.c
        self.b = self.z * 4 + self.X * 2 + self.Y

    def inner(self, k):
        yl, xl, c = flip(self.yl, k // 4), flip(self.xl, k // 2 % 2), flip(self.c, k % 2)
        e = (xor(xl, self.X) * 2 + xor(yl, self.Y)) * 2 + c
        return device(self.z, self.X, xl, self.Y, yl, c), yl * 4 + xl * 2 + c, e

    def row(self, k):
        X, Y, c = flip(self.X, k // 4), flip(self.Y, k // 2 % 2), flip(self.c, k % 2)
        return device(self.z, X, xor(self.gx, X), Y, xor(self.gy, Y), c), X * 4 + Y * 2 + c

    def taker(self, step, g):
        z = lax.rem(self.z + step + 8, 8)
        return device(z, self.xl, xor(self.xl, g // 2), self.yl, xor(self.yl, g % 2), self.c)

    def owner(self, w, step=0):
        return device(lax.rem(self.z + step + 8, 8), w // 2, self.X, w % 2, self.Y, self.c)

    def plane(self, step):
        return {"ctx": lax.rem(self.z + step + 8, 8) * 8 + self.X * 4 + self.Y * 2 + self.yl}

    def barrier(self):
        sem = pltpu.get_barrier_semaphore()

        def greet(to):
            pl.semaphore_signal(sem, inc=1, device_id=to, device_id_type=MESH)

        for step in (2, -2, 1, -1, 0):
            z = lax.rem(self.z + step + 8, 8)
            for i in range(1, 4):
                greet(device(z, self.xl, flip(self.X, i // 2), self.yl, flip(self.Y, i % 2), self.c))
                greet(device(z, flip(self.xl, i // 2), self.X, flip(self.yl, i % 2), self.Y, self.c))
            if step:
                greet(device(z, self.xl, self.X, self.yl, self.Y, self.c))
                greet(self.plane(step))
        for k in range(2, 8):
            greet(self.row(k)[0])
        for k in range(1, 8):
            greet(self.inner(k)[0])
        swapped = device(self.z, self.xl, self.X, self.yl, self.Y, self.c)
        here = (self.xl == self.X) & (self.yl == self.Y)

        @pl.when(jnp.logical_not(here))
        def _():
            greet(swapped)

        return lambda: pl.semaphore_wait(sem, 52 - here.astype(jnp.int32))


def device(z, X, xl, Y, yl, c):
    return {"ctx": z * 8 + X * 4 + Y * 2 + yl, "head": xl * 2 + c}


def remote(src, dst, send, recv, to):
    return pltpu.make_async_remote_copy(
        src_ref=src, dst_ref=dst, send_sem=send, recv_sem=recv, device_id=to, device_id_type=MESH
    )


def dot(a, b, contract):
    return lax.dot_general(a, b, ((contract[:1], contract[1:]), ((), ())), preferred_element_type=F32)


def terms(q, o, lse, delta, k, v, mask):
    scores = dot(k, q, (1, 1)) * (SCALE * LOG2E)
    weights = jnp.exp2(scores - lse)
    if mask is not None:
        weights = jnp.where(mask, weights, 0.0)
    slopes = weights * (dot(v, o, (1, 1)) - delta)
    return weights.astype(BF16), slopes.astype(BF16)


def kernel(
    gate_hbm,
    q_ref,
    o_ref,
    k_hbm,
    v_hbm,
    l_hbm,
    d_hbm,
    out_q,
    out_k,
    out_v,
    gate_ref,
    tab,
    k_ref,
    v_ref,
    ld_ref,
    sum_k,
    sum_v,
    q_in,
    o_in,
    own_kv,
    ld_in,
    kvl,
    kvz_0,
    kvz_1,
    picked,
    gkv,
    gate_out,
    gate_in,
    own_out,
    own_in,
    dq_sum,
    dq_out,
    run,
    z_out,
    z_in,
    end_out,
    end_in,
    far_in,
    q_send,
    q_recv,
    ld_send,
    ld_recv,
    n_send,
    n_recv,
    z_send,
    z_recv,
    r_send,
    r_recv,
    b_send,
    b_recv,
    g_send,
    g_recv,
    s_send,
    s_recv,
    e_send,
    e_recv,
    f_send,
    f_recv,
    l_sem,
    i_sem,
    o_sem,
):
    kvz = (kvz_0, kvz_1)
    me = Place()
    first = ((k_hbm, k_ref), (v_hbm, v_ref), (gate_hbm, gate_ref))
    first += ((l_hbm, ld_ref.at[pl.ds(0, 8)]), (d_hbm, ld_ref.at[pl.ds(8, 8)]))
    first = [pltpu.make_async_copy(a, b, i_sem.at[n]) for n, (a, b) in enumerate(first)]
    for copy in first:
        copy.start()
    everyone_is_here = me.barrier()
    for i in range(PARTS):
        run[i, 32] = jnp.zeros((PART, 256), F32)
    for copy in first:
        copy.wait()
    for g in range(4):
        kvl[g, :, :128] = k_ref[:, g * 128 : (g + 1) * 128]
        kvl[g, :, 128:] = v_ref[:, g * 128 : (g + 1) * 128]
    everyone_is_here()

    staying = (me.xl == me.X) & (me.yl == me.Y)
    sent = []
    maybe_sent = []

    def start(copy, here=None, local=None):
        if here is None:
            copy.start()
            sent.append(copy)
            return

        @pl.when(here)
        def _():
            local()

        @pl.when(jnp.logical_not(here))
        def _():
            copy.start()

        maybe_sent.append((here, copy))

    def await_part(part, send, recv, here=None):
        copy = remote(part, part, send, recv, me.plane(1))
        if here is None:
            copy.wait_recv()
            return

        @pl.when(jnp.logical_not(here))
        def _():
            copy.wait_recv()

    slot = me.X * 2 + me.Y
    STEPS = (1, -1, 0)
    for i in range(2):
        for n, step in enumerate(STEPS):
            for g in range(4):
                copy = remote(
                    kvl.at[g, pl.ds(i * HALF, HALF)],
                    kvz[i].at[me.b],
                    n_send.at[n, g, i],
                    n_recv.at[n, slot, i],
                    me.taker(step, g),
                )
                if step == 0 and g == 0:

                    def keep():
                        kvz[i][me.b] = kvl[0, i * HALF : (i + 1) * HALF]

                    start(copy, staying, keep)
                else:
                    start(copy)

    for k in range(1, 8):
        to, _, e = me.inner(k)
        start(remote(kvl.at[e // 2], own_kv.at[me.s], q_send.at[2, k], q_recv.at[2, k], to))
    ld_yl = xor(me.c, me.Y)
    ld_xl = xor(me.xl, me.X)
    for core in range(2):
        to = device(me.z, me.X, ld_xl, me.Y, ld_yl, core)
        here = (ld_xl == me.xl) & (ld_yl == me.yl) & (me.c == core)

        def keep():
            ld_in[me.yl] = ld_ref[...]

        start(
            remote(ld_ref, ld_in.at[me.yl], ld_send.at[core], ld_recv.at[me.yl], to), here, keep
        )
    for k in range(7, 0, -1):
        to, _, e = me.inner(k)
        cols = pl.ds(pl.multiple_of(e * 512, 512), 512)
        for i, (src, dst) in enumerate(((q_ref, q_in), (o_ref, o_in))):
            start(remote(src.at[:, cols], dst.at[me.s], q_send.at[i, k], q_recv.at[i, k], to))
    my_cols = pl.ds(pl.multiple_of(me.e * 512, 512), 512)
    local = [
        pltpu.make_async_copy(src.at[:, my_cols], dst.at[me.s], l_sem.at[i])
        for i, (src, dst) in enumerate(((q_ref, q_in), (o_ref, o_in)))
    ]
    for copy in local:
        copy.start()
    own_kv[me.s] = kvl[me.g]

    def fill(j, carry):
        tab[0, j] = gate_ref[me.z * 4 + j // 8, me.g * 8 + lax.rem(j, 8)]
        return carry

    def link(j, carry):
        mine = tab[0, j]
        previous, last = jnp.int32(32), jnp.int32(32)
        for other in range(32):
            gate = tab[0, other]
            previous = jnp.where((gate == mine) & (other < j), other, previous)
            last = jnp.where(gate == j, other, last)
        tab[1, j] = previous
        tab[2, j] = last
        return carry

    lax.fori_loop(0, 32, fill, 0)

    def chunk(d, i, first, count):
        return kvz[i].at[pl.ds(lax.rem(d + 8, 8) * 4 + first, count)]

    def span(way, t):
        return (way * 2, 2) if t == 3 else (0, 4)

    def pass_on(way, t, i):
        sign = 1 - 2 * way
        part = chunk(me.z - sign * t, i, *span(way, t))
        start(remote(part, part, z_send.at[way, t, i], z_recv.at[way, t, i], me.plane(sign)))

    def arrived(way, t, i):
        part = chunk(me.z - (1 - 2 * way) * (t + 1), i, *span(way, t))
        await_part(part, z_send.at[way, t, i], z_recv.at[way, t, i])

    def arrived_first(n, i):
        for w in range(4):
            block = kvz[i].at[lax.rem(me.z - STEPS[n] + 8, 8) * 4 + w]
            here = staying & (slot == w) if n == 2 else None
            await_part(block, n_send.at[n, 0, i], n_recv.at[n, w, i], here)

    def pick(i):
        for k in (7, 6, 5, 4, 3, 2, 1, 0):
            to, p = me.row(k)
            for h in range(4):
                got = kvz[i // 2][tab[0, p * 4 + h], i % 2 * PART : (i % 2 + 1) * PART]
                if k == 0:
                    gkv[i, me.m, h] = got
                else:
                    picked[i, k, h] = got
            if k:
                start(
                    remote(picked.at[i, k], gkv.at[i, me.m], r_send.at[i, k], r_recv.at[i, k], to)
                )

    def both(what, *args):
        for way in range(2):
            what(*args[:-2], way, *args[-2:])

    for i in range(2):
        for way in range(2):
            arrived_first(way, i)
            pass_on(way, 1, i)
    for t in (2, 3):
        for i in range(2):
            for way in range(2):
                arrived(way, t - 1, i)
                pass_on(way, t, i)
    for i in range(2):
        arrived_first(2, i)
        both(arrived, 3, i)
        pick(2 * i)
        pick(2 * i + 1)
    lax.fori_loop(0, 32, link, 0)

    for copy in local:
        copy.wait()
    for k in range(1, 8):
        _, s, _ = me.inner(k)
        for i, dst in enumerate((q_in, o_in, own_kv)):
            await_part(dst.at[s], q_send.at[i, k], q_recv.at[i, k])
    for yl in range(2):
        here = (me.gx == me.xl) & (me.gy == me.c) & (me.yl == yl)
        await_part(ld_in.at[yl], ld_send.at[0], ld_recv.at[yl], here)

    def rows_of(h):
        row = 4 * me.c + h
        lse = jnp.concatenate([ld_in[i, pl.ds(row, 1), :] for i in range(2)], axis=1) * LOG2E
        delta = jnp.concatenate([ld_in[i, pl.ds(row + 8, 1), :] for i in range(2)], axis=1)
        lanes = slice(h * 128, (h + 1) * 128)
        q = q_in[:, :, lanes].reshape(512, 128)
        o = o_in[:, :, lanes].reshape(512, 128)
        return q, o, lse, delta

    TILE = 256
    key_pos = lax.broadcasted_iota(jnp.int32, (TILE, TILE), 0)
    query_pos = lax.broadcasted_iota(jnp.int32, (TILE, TILE), 1)
    causal = key_pos <= query_pos
    own = own_kv[...].reshape(512, 256)
    own_k, own_v = own[:, :128], own[:, 128:]
    own_dk = [jnp.zeros((TILE, 128), F32) for _ in range(2)]
    own_dv = [jnp.zeros((TILE, 128), F32) for _ in range(2)]
    for h in range(4):
        q, o, lse, delta = rows_of(h)
        for i in range(2):
            cols = slice(i * TILE, (i + 1) * TILE)
            dq = jnp.zeros((TILE, 128), F32)
            for j in range(i + 1):
                keys = slice(j * TILE, (j + 1) * TILE)
                mask = causal if i == j else None
                w, s = terms(
                    q[cols], o[cols], lse[:, cols], delta[:, cols], own_k[keys], own_v[keys], mask
                )
                own_dv[j] += dot(w, o[cols], (1, 0))
                own_dk[j] += dot(s, q[cols], (1, 0))
                dq += dot(s, own_k[keys], (0, 0))
            dq_sum[h, cols] = dq
    for j in range(2):
        part = jnp.concatenate([own_dk[j] * SCALE, own_dv[j]], axis=1).astype(BF16)
        own_out[j * 4 : (j + 1) * 4] = part.reshape(4, 64, 256)
    for k in range(1, 8):
        to, s, _ = me.inner(k)
        start(remote(own_out.at[s], own_in.at[me.e], q_send.at[3, k], q_recv.at[3, k], to))
    own_in[me.e] = own_out[me.s]

    keys = 8 * PART
    for group in GROUPS:
        for part in group:
            for k in range(1, 8):
                _, p = me.row(k)
                await_part(gkv.at[part, p], r_send.at[part, k], r_recv.at[part, k])
        for h in range(4):
            q, o, lse, delta = rows_of(h)
            lse = jnp.where(tab[0, me.m * 4 + h] != me.b, lse, 1e30)
            kv = [gkv[part, :, h].reshape(keys, 256) for part in group]
            kv = kv[0] if len(kv) == 1 else jnp.concatenate(kv, axis=0)
            k_rows, v_rows = kv[:, :128], kv[:, 128:]
            dk = jnp.zeros((len(group) * keys, 128), F32)
            dv = jnp.zeros((len(group) * keys, 128), F32)
            for j in range(2):
                cols = slice(j * TILE, (j + 1) * TILE)
                w, s = terms(q[cols], o[cols], lse[:, cols], delta[:, cols], k_rows, v_rows, None)
                dv += dot(w, o[cols], (1, 0))
                dk += dot(s, q[cols], (1, 0))
                dq = dq_sum[h, cols] + dot(s, k_rows, (0, 0))
                if group[-1] < PARTS - 1:
                    dq_sum[h, cols] = dq
                else:
                    piece = (dq * SCALE).astype(BF16).reshape(4, 64, 128)
                    dq_out[j * 4 : (j + 1) * 4, :, h * 128 : (h + 1) * 128] = piece
            both_k_v = jnp.concatenate([dk * SCALE, dv], axis=1).astype(BF16)
            for n, part in enumerate(group):
                gate_out[part, :, h] = both_k_v[n * keys : (n + 1) * keys].reshape(8, PART, 256)
        for part in group:
            for k in (7, 6, 5, 4, 3, 2, 1):
                to, p = me.row(k)
                src, dst = gate_out.at[part, p], gate_in.at[part, me.m]
                start(remote(src, dst, b_send.at[part, k], b_recv.at[part, k], to))
            gate_in[part, me.m] = gate_out[part, me.m]
    for k in range(1, 8):
        to, s, _ = me.inner(k)
        start(remote(dq_out.at[s], out_q.at[:, my_cols], g_send.at[k], g_recv.at[k], to))
    dq_local = pltpu.make_async_copy(dq_out.at[me.s], out_q.at[:, my_cols], l_sem.at[0])
    dq_local.start()

    def add_up(i):
        for k in range(1, 8):
            _, p = me.row(k)
            await_part(gate_in.at[i, p], b_send.at[i, k], b_recv.at[i, k])

        def add(j, carry):
            run[i, j] = gate_in[i, j // 4, lax.rem(j, 4)].astype(F32) + run[i, tab[1, j]]
            return carry

        lax.fori_loop(0, 32, add, 0)

    def total(i, d, w):
        return run[i, tab[2, lax.rem(d + 8, 8) * 4 + w]]

    HOPS = (1, 2, 1, 2)

    def sum_on(way, t, i):
        sign = 1 - 2 * way
        first, count = span(way, t)
        for w in range(first, first + count):
            value = total(i, me.z + sign * (t + 1), w)
            if t == 1:
                value += z_in[way, 2, i, w].astype(F32)
                if way * 2 <= w < way * 2 + 2:
                    value += z_in[way, 3, i, w].astype(F32)
            z_out[way, t, i, w] = value.astype(BF16)
        if t < 2 and i == PARTS - 1:
            for w in range(4):
                dst = far_in.at[way, t, me.g]
                to = me.owner(w, sign * HOPS[t])
                start(
                    remote(z_out.at[way, t, i, w], dst, f_send.at[way, t, w], f_recv.at[way, t, me.g], to)
                )
            return
        src = z_out.at[way, t, i, pl.ds(first, count)]
        dst = z_in.at[way, t, i, pl.ds(first, count)]
        to = me.plane(sign * HOPS[t])
        start(remote(src, dst, s_send.at[way, t, i], s_recv.at[way, t, i], to))

    def sum_arrived(way, t, i):
        part = z_in.at[way, t, i, pl.ds(*span(way, t))]
        await_part(part, s_send.at[way, t, i], s_recv.at[way, t, i])

    def middle(i):
        for way in range(2):
            sum_arrived(way, 2, i)
            sum_arrived(way, 3, i)
            sum_on(way, 1, i)

    def sum_here(i):
        far = i == PARTS - 1
        for t in range(0 if far else 2):
            both(sum_arrived, t, i)
        for w in range(4):
            value = total(i, me.z, w)
            for way in range(0 if far else 2):
                value += z_in[way, 0, i, w].astype(F32) + z_in[way, 1, i, w].astype(F32)
            end_out[i, w] = value
            copy = remote(
                end_out.at[i, w],
                end_in.at[me.g, i],
                e_send.at[w, i],
                e_recv.at[me.g, i],
                me.owner(w),
            )

            def keep():
                end_in[0, i] = end_out[i, w]

            start(copy, staying & (slot == w), keep)

    for i in range(PARTS):
        add_up(i)
        for t in (3, 2, 0):
            both(sum_on, t, i)
        if i >= 1:
            middle(i - 1)
        if i >= 3:
            sum_here(i - 3)
    sum_here(PARTS - 1)
    sum_here(PARTS - 3)
    middle(PARTS - 1)
    sum_here(PARTS - 2)

    for k in range(1, 8):
        _, _, e = me.inner(k)
        await_part(own_in.at[e], q_send.at[3, k], q_recv.at[3, k])
    results = []
    for i in range(PARTS):
        toks = slice(i * PART, (i + 1) * PART)
        for g in range(4):
            value = own_in[2 * g, toks].astype(F32) + own_in[2 * g + 1, toks].astype(F32)
            here = staying if g == 0 else None
            await_part(end_in.at[g, i], e_send.at[g, i], e_recv.at[g, i], here)
            value += end_in[g, i]
            if i == PARTS - 1:
                for way in range(2):
                    for t in range(2):
                        part = far_in.at[way, t, g]
                        await_part(part, f_send.at[way, t, g], f_recv.at[way, t, g])
                        value += far_in[way, t, g].astype(F32)
            sum_k[toks, g * 128 : (g + 1) * 128] = value[:, :128].astype(BF16)
            sum_v[toks, g * 128 : (g + 1) * 128] = value[:, 128:].astype(BF16)
        for n, (src, dst) in enumerate(((sum_k, out_k), (sum_v, out_v))):
            rows = pl.ds(i * PART, PART)
            results.append(pltpu.make_async_copy(src.at[rows], dst.at[rows], o_sem.at[n, i]))
            results[-1].start()

    for copy in [dq_local] + results:
        copy.wait()
    for k in range(1, 8):
        _, _, e = me.inner(k)
        part = out_q.at[:, pl.ds(pl.multiple_of(e * 512, 512), 512)]
        await_part(part, g_send.at[k], g_recv.at[k])
    for here, copy in maybe_sent:

        @pl.when(jnp.logical_not(here))
        def _():
            copy.wait_send()

    for copy in sent:
        copy.wait_send()


def hand_over(q, k, v, out_q, out_k, out_v, held_q, held_k, held_v, in_sem, out_sem):
    jobs = []
    for i in range(4):
        rows = pl.ds(i * 16, 16)
        jobs.append((q.at[rows], held_q.at[rows], out_q.at[rows]))
    jobs += [(k, held_k, out_k), (v, held_v, out_v)]
    arrivals = [pltpu.make_async_copy(a, b, in_sem.at[i]) for i, (a, b, _) in enumerate(jobs)]
    leavings = [pltpu.make_async_copy(b, c, out_sem.at[i]) for i, (_, b, c) in enumerate(jobs)]
    for copy in arrivals:
        copy.start()
    for arrival, leaving in zip(arrivals, leavings):
        arrival.wait()
        leaving.start()
    for copy in leavings:
        copy.wait()


HBM_SPEC = pl.BlockSpec(memory_space=pltpu.HBM)
DMA = pltpu.SemaphoreType.DMA
VMEM_LIMIT = 63 * 1024 * 1024


def shape(*dims, dtype=BF16):
    return jax.ShapeDtypeStruct(dims, dtype)


def shards(queries, keys, values, out_grad, lse, delta, gate_block):
    def buf(*dims, dtype=BF16):
        return pltpu.VMEM(dims, dtype)

    parts = pl.pallas_call(
        kernel,
        out_shape=(shape(64, 4096), shape(64, 512), shape(64, 512)),
        in_specs=[HBM_SPEC] * 7,
        out_specs=(HBM_SPEC,) * 3,
        scratch_shapes=[
            pltpu.SMEM((32, 32), jnp.int32),
            pltpu.SMEM((3, 32), jnp.int32),
            buf(64, 512),
            buf(64, 512),
            buf(16, 256, dtype=F32),
            buf(64, 512),
            buf(64, 512),
            buf(8, 64, 512),
            buf(8, 64, 512),
            buf(8, 64, 256),
            buf(2, 16, 256, dtype=F32),
            buf(4, 64, 256),
            buf(32, HALF, 256),
            buf(32, HALF, 256),
            buf(PARTS, 8, 4, PART, 256),
            buf(PARTS, 8, 4, PART, 256),
            buf(PARTS, 8, 4, PART, 256),
            buf(PARTS, 8, 4, PART, 256),
            buf(8, 64, 256),
            buf(8, 64, 256),
            buf(4, 512, 128, dtype=F32),
            buf(8, 64, 512),
            buf(PARTS, 33, PART, 256, dtype=F32),
            buf(2, 4, PARTS, 4, PART, 256),
            buf(2, 4, PARTS, 4, PART, 256),
            buf(PARTS, 4, PART, 256, dtype=F32),
            buf(4, PARTS, PART, 256, dtype=F32),
            buf(2, 2, 4, PART, 256),
            DMA((4, 8)),
            DMA((4, 8)),
            DMA((2,)),
            DMA((2,)),
            DMA((3, 4, 2)),
            DMA((3, 4, 2)),
            DMA((2, 4, 2)),
            DMA((2, 4, 2)),
            DMA((PARTS, 8)),
            DMA((PARTS, 8)),
            DMA((PARTS, 8)),
            DMA((PARTS, 8)),
            DMA((8,)),
            DMA((8,)),
            DMA((2, 4, PARTS)),
            DMA((2, 4, PARTS)),
            DMA((4, PARTS)),
            DMA((4, PARTS)),
            DMA((2, 2, 4)),
            DMA((2, 2, 4)),
            DMA((2,)),
            DMA((5,)),
            DMA((2, PARTS)),
        ],
        compiler_params=pltpu.CompilerParams(
            collective_id=0, has_side_effects=True, vmem_limit_bytes=VMEM_LIMIT
        ),
        name="block_attention_backward",
    )(gate_block, queries, out_grad, keys, values, lse.T, delta.T)
    return pl.pallas_call(
        hand_over,
        out_shape=(shape(64, 4096), shape(64, 512), shape(64, 512)),
        in_specs=[HBM_SPEC] * 3,
        out_specs=(HBM_SPEC,) * 3,
        scratch_shapes=[buf(64, 4096), buf(64, 512), buf(64, 512), DMA((6,)), DMA((6,))],
        compiler_params=pltpu.CompilerParams(vmem_limit_bytes=VMEM_LIMIT),
        name="hand_over",
    )(*parts)


def solution(mesh):
    rows = P(("ctx", "head"), None)
    return jax.shard_map(
        shards,
        mesh=mesh,
        in_specs=(rows, rows, rows, rows, P("ctx", "head"), P("ctx", "head"), P()),
        out_specs=(rows, rows, rows),
        check_vma=False,
    )
```
